128 devices in a mesh: seq: 16 (over y, z_lo, core), tp: 8 (over x, z_hi).
Axes of the slice: x: 4, y: 4, z: 4 (z_hi: 2, z_lo: 2; z = z_hi * 2 + z_lo), core: 2. Of those that a mesh axis runs over, the one named last changes fastest.
Arguments:
- tokens: bfloat16 [16384, 2560], P('seq'), may hold values from -6 to 6
- visible: int32 [16384], P('seq'), may hold values from 0 to 1, as said below
- w_in: bfloat16 [2560, 10240], P(None, 'tp'), may hold values from -0.125 to 0.125
- w_out: bfloat16 [10240, 2560], P('tp'), may hold values from -0.0625 to 0.0625
- w_query: bfloat16 [2560, 2048], P(None, 'tp'), may hold values from -4 to 4
- w_key: bfloat16 [2560, 2048], P(None, 'tp'), may hold values from -1 to 1
- w_value: bfloat16 [2560, 2048], P(None, 'tp'), may hold values from -0.125 to 0.125
- w_proj: bfloat16 [2048, 2560], P('tp'), may hold values from -3 to 3
Outputs:
- mixed: float32 [16384, 2560], P('seq', 'tp')
The draws below stay inside these ranges and needn't reach their ends.
Inputs may be any that keep to these rules, and one draw needn't show every extreme that they name: Among the 1024 positions of each index of seq at most 768 are visible, and some index has exactly 768; exactly 4096 positions are visible in all.
All inputs are finite; a program needn't handle non-finite values.
Results may differ from the reference program's by a relative error of at most 0.04.
Values may be sent and summed in bfloat16 or wider, within the bound.
A program may use at most 256 MiB of HBM per device.

```python
import math
import jax
import jax.numpy as jnp
from jax import lax

D = 2560
FF = 10240
HEADS = 16
HEAD_DIM = 128
TOK_DEV = 1024
TOKENS = 16384
VIS_TOTAL = 4096
N_TP = 8


def shared_weight(key):
    base = jax.random.normal(key, (D, HEADS * HEAD_DIM), jnp.float32)
    return jnp.clip(base, -6.0, 6.0) * D ** (-0.5)


def draw_w_key(key, part):
    base = shared_weight(key)
    return base.astype(jnp.bfloat16)


def draw_w_query(key, part):
    key = jax.random.fold_in(key, 13)
    noise = jnp.clip(jax.random.normal(key, (D, HEADS * HEAD_DIM), jnp.float32), -6.0, 6.0) * D ** (-0.5)
    result = noise
    return result.astype(jnp.bfloat16)


def draw_w_proj(key, part):
    key = jax.random.fold_in(key, 17)
    fan_in = HEADS * HEAD_DIM
    column = jnp.arange(D, dtype=jnp.float32) / (D - 1)
    base = jnp.clip(jax.random.normal(key, (fan_in, D), jnp.float32), -6.0, 6.0)
    rise = jnp.exp(math.log(4.0) * column)
    return (base * rise[None, :] * fan_in ** (-0.5)).astype(jnp.bfloat16)


def draw_tokens(key, part):
    key = jax.random.fold_in(key, 3)
    result = jax.random.normal(key, (TOKENS, D), jnp.float32)
    return jnp.clip(result, -6.0, 6.0).astype(jnp.bfloat16)


def draw_visible(key, part):
    key = jax.random.fold_in(key, 5)
    shard_total = TOKENS // TOK_DEV
    order_key, amount_key, place_key = jax.random.split(key, 3)
    order = jax.random.permutation(order_key, shard_total)
    standing = jnp.argsort(order, stable=True).astype(jnp.int32)
    mean_count = TOK_DEV // 4
    most = 3 * TOK_DEV // 4
    remainder = standing - 3
    pair_index = jnp.clip(remainder // 2, 0, shard_total - 1)
    amounts = jax.random.randint(amount_key, (shard_total,), 0, mean_count + 1)
    taken = amounts[pair_index]
    paired = 2 * (remainder // 2) + 1 < shard_total - 3
    signed = jnp.where(remainder % 2 == 0, taken, -taken)
    delta = jnp.where(paired, signed, 0)
    counts = jnp.where(standing == 0, most, jnp.where(standing < 3, 0, mean_count + delta))
    shard_keys = jax.random.split(place_key, shard_total)
    places = jax.vmap(lambda one_key: jax.random.permutation(one_key, TOK_DEV))(shard_keys)
    return (places < counts[:, None]).astype(jnp.int32).reshape(TOKENS)


def block_levels(key, dims, cuts, smallest, high):
    def one(position, parts):
        steps = jax.random.uniform(jax.random.fold_in(jax.random.fold_in(key, 6), position), (parts,), jnp.float32, smallest / len(cuts), high / len(cuts))
        return jnp.repeat(jnp.exp(steps), dims[position] // parts).reshape((-1,) + (1,) * (len(dims) - position - 1))

    gain = one(*cuts[0])
    for cut in cuts[1:]:
        gain = gain * one(*cut)
    return gain


def bell_draw(key, dims, scale, bound, shards=(), held_as=jnp.bfloat16):
    gain = block_levels(key, dims, shards, -0.22, 0.18) if shards else 1.0
    array = jax.random.normal(key, dims, jnp.float32) * scale * gain
    return jnp.minimum(jnp.maximum(array, -bound), bound).astype(held_as)


def setup_inputs(seed: int = 0) -> dict:
    seeds = jax.random.split(jax.random.key(seed), 9)
    return {
        "tokens": draw_tokens(jax.random.fold_in(seeds[8], 71), 0),
        "visible": draw_visible(jax.random.fold_in(seeds[8], 71), 0),
        "w_in": bell_draw(seeds[2], (D, FF), D ** -0.5, 0.125, ((1, 8),)),
        "w_out": bell_draw(seeds[3], (FF, D), FF ** -0.5, 0.0625, ((0, 8),)),
        "w_query": draw_w_query(jax.random.fold_in(seeds[8], 71), 0),
        "w_key": draw_w_key(jax.random.fold_in(seeds[8], 71), 0),
        "w_value": bell_draw(seeds[6], (D, HEADS * HEAD_DIM), D ** -0.5, 0.125, ((1, 8),)),
        "w_proj": draw_w_proj(jax.random.fold_in(seeds[8], 71), 0),
    }


def norm_rows(values):
    row_mean = lax.optimization_barrier(jnp.mean(values, axis=-1, keepdims=True))
    centred = values - row_mean
    variance = lax.optimization_barrier(jnp.mean(centred * centred, axis=-1, keepdims=True))
    return centred * lax.rsqrt(variance + 1e-05)

def rounded_term(term):
    return lax.optimization_barrier(term.astype(jnp.bfloat16)).astype(jnp.float32)

def reference(tokens, visible, w_in, w_out, w_query, w_key, w_value, w_proj):
    normed = norm_rows(tokens.astype(jnp.float32)).astype(jnp.bfloat16)
    where_vis = jnp.nonzero(visible > 0, size=VIS_TOTAL)[0].astype(jnp.int32)
    vis_norm = normed[where_vis]
    vis_tok = tokens[where_vis]
    group = FF // N_TP
    ffn_total = jnp.zeros((VIS_TOTAL, D), jnp.float32)
    for index in range(N_TP):
        hidden = jax.nn.gelu(jnp.dot(vis_norm, w_in[:, index * group:(index + 1) * group], preferred_element_type=jnp.float32)).astype(jnp.bfloat16)
        ffn_total = ffn_total + rounded_term(jnp.dot(hidden, w_out[index * group:(index + 1) * group], preferred_element_type=jnp.float32))
    encoded = (vis_tok.astype(jnp.float32) + ffn_total).astype(jnp.bfloat16)
    key_in = norm_rows(encoded.astype(jnp.float32)).astype(jnp.bfloat16)
    key_rows = jnp.dot(key_in, w_key, preferred_element_type=jnp.float32).astype(jnp.bfloat16).reshape(VIS_TOTAL, HEADS, HEAD_DIM)
    value_rows = jnp.dot(key_in, w_value, preferred_element_type=jnp.float32).astype(jnp.bfloat16).reshape(VIS_TOTAL, HEADS, HEAD_DIM)
    queries = jnp.dot(normed, w_query, preferred_element_type=jnp.float32).astype(jnp.bfloat16)
    block = 512
    score_scale = HEAD_DIM ** (-0.5)
    key_float = key_rows.astype(jnp.float32)
    value_float = value_rows.astype(jnp.float32)

    def attend(query_block):
        scores = jnp.einsum('qhd,khd->hqk', query_block.astype(jnp.float32), key_float) * score_scale
        top = lax.optimization_barrier(jnp.max(scores, axis=-1, keepdims=True))
        weights = jnp.exp(scores - top).astype(jnp.bfloat16)
        totals = lax.optimization_barrier(jnp.sum(weights.astype(jnp.float32), axis=-1))
        summed = jnp.einsum('hqk,khd->qhd', weights.astype(jnp.float32), value_float)
        return (summed / jnp.transpose(totals)[:, :, None]).astype(jnp.bfloat16)
    attended = lax.map(attend, queries.reshape(TOKENS // block, block, HEADS, HEAD_DIM))
    attended = attended.reshape(TOKENS, HEADS * HEAD_DIM)
    head_group = HEADS * HEAD_DIM // N_TP
    projected = jnp.zeros((TOKENS, D), jnp.float32)
    for index in range(N_TP):
        projected = projected + rounded_term(jnp.dot(attended[:, index * head_group:(index + 1) * head_group], w_proj[index * head_group:(index + 1) * head_group], preferred_element_type=jnp.float32))
    return tokens.astype(jnp.float32) + norm_rows(projected)
```

```python
import functools
import math

import jax
import jax.numpy as jnp
from jax import lax
from jax.experimental import pallas as pl
from jax.experimental.pallas import tpu as pltpu
from jax.sharding import PartitionSpec as P

HEAD_DIM = 128
EPSILON = 1e-05
MESH = pl.DeviceIdType.MESH
F32 = jnp.float32
BF16 = jnp.bfloat16
N_SEQ = 16
N_TP = 8
LAST_PHASE = 9


def norm_rows(values):
    row_mean = jnp.mean(values, axis=-1, keepdims=True)
    centred = values - row_mean
    variance = jnp.mean(centred * centred, axis=-1, keepdims=True)
    return centred * lax.rsqrt(variance + EPSILON)


def dot(a, b):
    return jnp.dot(a, b, preferred_element_type=F32)


def dot_t(a, b):
    return lax.dot_general(a, b, (((1,), (1,)), ((), ())), preferred_element_type=F32)


class Sems:
    def __init__(self, send, recv):
        self.send, self.recv, self.used = send, recv, 0

    def take(self, count):
        first = self.used
        self.used += count
        return first


class RingGather:
    def __init__(self, sems, ring, pair, block, device):
        self.sems, self.ring, self.pair = sems, ring, pair
        self.block, self.device = block, device
        self.base = sems.take(9)
        self.sent = []

    def _copy(self, i, ref, device):
        return pltpu.make_async_remote_copy(
            src_ref=ref,
            dst_ref=ref,
            send_sem=self.sems.send.at[self.base + i],
            recv_sem=self.sems.recv.at[self.base + i],
            device_id=device,
            device_id_type=MESH,
        )

    def _send(self, i, ring, pair, half, to_ring, to_pair):
        copy = self._copy(i, self.block(ring, pair, half), self.device(to_ring, to_pair))
        copy.start()
        self.sent.append(copy)

    def _wait(self, i, ring, pair, half):
        self._copy(i, self.block(ring, pair, half), self.device(self.ring, 1 - self.pair)).wait_recv()

    def start(self):
        r, p = self.ring, self.pair
        self._send(0, r, p, None, r, 1 - p)
        self._send(1, r, p, None, r + 1, p)
        self._send(2, r, p, None, r + 3, p)

    def partner(self):
        r, p = self.ring, self.pair
        self._wait(0, r, 1 - p, None)
        self._send(3, r, 1 - p, None, r + 1, p)
        self._send(4, r, 1 - p, None, r + 3, p)

    def sides(self):
        r, p = self.ring, self.pair
        self._wait(1, r + 3, p, None)
        self._send(5, r + 3, p, 0, r + 1, p)
        self._wait(2, r + 1, p, None)
        self._send(6, r + 1, p, 1, r + 3, p)

    def partner_sides(self):
        r, p = self.ring, self.pair
        self._wait(3, r + 3, 1 - p, None)
        self._send(7, r + 3, 1 - p, 0, r + 1, p)
        self._wait(4, r + 1, 1 - p, None)
        self._send(8, r + 1, 1 - p, 1, r + 3, p)

    def far(self):
        self._wait(5, self.ring + 2, self.pair, 0)
        self._wait(6, self.ring + 2, self.pair, 1)

    def partner_far(self):
        self._wait(7, self.ring + 2, 1 - self.pair, 0)
        self._wait(8, self.ring + 2, 1 - self.pair, 1)

    def drain(self):
        for copy in self.sent:
            copy.wait_send()


class CoreShare:
    def __init__(self, sems, block, core, device):
        self.sems, self.block, self.core, self.device = sems, block, core, device
        self.base = sems.take(8)
        self.sent = []

    def _copy(self, i, ring, pair, core):
        ref = self.block(ring, pair, core)
        return pltpu.make_async_remote_copy(
            src_ref=ref,
            dst_ref=ref,
            send_sem=self.sems.send.at[self.base + i],
            recv_sem=self.sems.recv.at[self.base + i],
            device_id=self.device,
            device_id_type=MESH,
        )

    def send(self, i, ring, pair):
        copy = self._copy(i, ring, pair, self.core)
        copy.start()
        self.sent.append(copy)

    def wait(self, i, ring, pair):
        self._copy(i, ring, pair, 1 - self.core).wait_recv()

    def drain(self):
        for copy in self.sent:
            copy.wait_send()


def kernel(
    vis_tile,
    vis_row,
    tok_hbm,
    w_in_hbm,
    w_out_hbm,
    w_q_hbm,
    w_k_hbm,
    w_v_hbm,
    w_p_hbm,
    out_ref,
    tok,
    w_in,
    w_out,
    w_q,
    w_k,
    w_v,
    w_p,
    counts,
    pick_out,
    pick_in,
    own_rows,
    enc_in,
    hidden,
    part_out,
    part_in,
    key_in,
    kv,
    q_ref,
    top_ref,
    acc_ref,
    att_out,
    att_in,
    proj,
    res_out,
    local_sem,
    send_sem,
    recv_sem,
):
    rows, width = tok.shape
    seq = lax.axis_index("seq")
    tp = lax.axis_index("tp")
    core, z_lo, y = seq % 2, (seq // 2) % 2, seq // 4
    x, z_hi = tp // 2, tp % 2
    sems = Sems(send_sem, recv_sem)
    vis_here = width // N_TP // 10
    vis_here = own_rows.shape[0]
    group = vis_here * N_TP
    half_width = width // 2

    def at_seq(index):
        return {"seq": index, "tp": tp}

    def at_tp(index):
        return {"seq": seq, "tp": index}

    def seq_of(ring, pair, which):
        return ((ring % 4) * 2 + pair) * 2 + which

    def tp_of(ring, pair):
        return (ring % 4) * 2 + pair

    locals_ = []
    for i, (src, dst) in enumerate(
        (
            (tok_hbm, tok),
            (w_q_hbm, w_q),
            (w_in_hbm, w_in),
            (w_out_hbm, w_out),
            (w_k_hbm, w_k),
            (w_v_hbm, w_v),
        )
    ):
        copy = pltpu.make_async_copy(src, dst, local_sem.at[i])
        copy.start()
        locals_.append(copy)
    got_tok, got_q, got_in, got_out, got_k, got_v = locals_
    slice_rows = w_p.shape[1] // N_SEQ
    own_slice = pl.ds(pl.multiple_of(seq * slice_rows, slice_rows), slice_rows)
    got_p = pltpu.make_async_copy(w_p_hbm.at[own_slice], w_p.at[tp, own_slice], local_sem.at[6])
    got_p.start()

    barrier = pltpu.get_barrier_semaphore()

    @pl.loop(1, N_SEQ)
    def _(d):
        pl.semaphore_signal(
            barrier, inc=1, device_id=at_seq((seq + d) % N_SEQ), device_id_type=MESH
        )

    @pl.loop(1, N_TP)
    def _(d):
        pl.semaphore_signal(barrier, inc=1, device_id=at_tp((tp + d) % N_TP), device_id_type=MESH)

    pl.semaphore_wait(barrier, N_SEQ + N_TP - 2)

    def remote(src, dst, index, device):
        return pltpu.make_async_remote_copy(
            src_ref=src,
            dst_ref=dst,
            send_sem=send_sem.at[index],
            recv_sem=recv_sem.at[index],
            device_id=device,
            device_id_type=MESH,
        )

    count_base = sems.take(N_SEQ)

    @pl.loop(1, N_SEQ)
    def _(d):
        remote(
            vis_tile, counts.at[seq], count_base + d, at_seq((seq + d) % N_SEQ)
        ).start()

    counts[pl.ds(seq, 1)] = vis_tile[...][None]

    slice_base = sems.take(N_TP)

    @pl.loop(1, N_TP)
    def _(d):
        remote(
            w_p_hbm.at[own_slice], w_p.at[tp, own_slice], slice_base + d, at_tp((tp + d) % N_TP)
        ).start()

    visible = vis_row[...].astype(F32)
    lower = (
        lax.broadcasted_iota(jnp.int32, (rows, rows), 0)
        <= lax.broadcasted_iota(jnp.int32, (rows, rows), 1)
    ).astype(F32).astype(BF16)
    upto = dot(jnp.broadcast_to(visible, (8, rows)).astype(BF16), lower)[:1]

    @pl.loop(1, N_SEQ)
    def _(d):
        remote(
            vis_tile, counts.at[(seq + N_SEQ - d) % N_SEQ], count_base + d, at_seq((seq + d) % N_SEQ)
        ).wait()

    lane_source = lax.broadcasted_iota(jnp.int32, (1, 256), 1) // 16
    before_me = jnp.zeros((1, 1), F32)
    lane_before = jnp.zeros((1, 256), F32)
    lane_count = jnp.zeros((1, 256), F32)
    for s in range(N_SEQ):
        count = jnp.sum(counts[s].astype(F32), axis=1, keepdims=True)
        count = jnp.sum(count, axis=0, keepdims=True)
        before_me = before_me + jnp.where(seq > s, 1.0, 0.0) * count
        lane_before = lane_before + jnp.where(lane_source > s, count, 0.0)
        lane_count = lane_count + jnp.where(lane_source == s, count, 0.0)

    rank = (before_me + upto - 1.0).astype(jnp.int32)
    code = ((rank >> 3) & 15) * 8 + ((rank >> 7) & 7)
    code = jnp.where((visible > 0.0) & ((rank & 7) == tp), code, -1)
    picks = (lax.broadcasted_iota(jnp.int32, (128, rows), 0) == code).astype(F32).astype(BF16)
    got_tok.wait()
    for h in range(2):
        for c in range(0, half_width, 640):
            rows_of = dot(picks, tok[:, h * half_width + c : h * half_width + c + 640])
            rows_of = rows_of.reshape(16, 8, 640)
            if h == 0:
                proj[:, c : c + 640] = rows_of.reshape(128, 640)
            else:
                first = proj[:, c : c + 640].reshape(16, 8, 640)
                both = jnp.concatenate([first, rows_of], axis=1)
                pick_out[:, c : c + 640] = both.reshape(256, 640).astype(BF16)

    pick_base = sems.take(N_SEQ)

    def pick_rows(index):
        return pl.ds(pl.multiple_of(index * 16, 16), 16)

    @pl.loop(1, N_SEQ)
    def _(d):
        to = (seq + d) % N_SEQ
        remote(
            pick_out.at[pick_rows(to)], pick_in.at[pick_rows(seq)], pick_base + d, at_seq(to)
        ).start()

    pick_in[pick_rows(seq)] = pick_out[pick_rows(seq)]

    query_scale = HEAD_DIM ** (-0.5) * math.log2(math.e)
    got_q.wait()

    def make_queries(first, last):
        @pl.loop(first, last)
        def _(c):
            here = pl.ds(pl.multiple_of(c * 128, 128), 128)
            normed = norm_rows(tok[here].astype(F32)).astype(BF16)
            q_ref[here] = (dot(normed, w_q[...]) * query_scale).astype(BF16)

    make_queries(0, 4)

    @pl.loop(1, N_SEQ)
    def _(d):
        to = (seq + d) % N_SEQ
        source = (seq + N_SEQ - d) % N_SEQ
        remote(
            pick_out.at[pick_rows(to)], pick_in.at[pick_rows(source)], pick_base + d, at_seq(to)
        ).wait()

    slot = lax.broadcasted_iota(jnp.int32, (vis_here, 256), 0)
    lane = lax.broadcasted_iota(jnp.int32, (vis_here, 256), 1)
    wanted = (slot * 128 + seq * 8 + tp).astype(F32)
    live = (wanted >= lane_before) & (wanted < lane_before + lane_count)
    live = live & ((lane & 7) == (slot & 7))
    for h in range(2):
        chosen = (live & (((lane >> 3) & 1) == h)).astype(F32).astype(BF16)
        own_rows[:, h * half_width : (h + 1) * half_width] = dot(chosen, pick_in[...])

    def own_block(ref, ring, pair, half):
        first = tp_of(ring, pair) * vis_here
        if half is None:
            return ref.at[pl.ds(pl.multiple_of(first, vis_here), vis_here)]
        part = vis_here // 2
        return ref.at[pl.ds(pl.multiple_of(first + half * part, part), part)]

    def tp_device(ring, pair):
        return at_tp(tp_of(ring, pair))

    mine = pl.ds(pl.multiple_of(tp * vis_here, vis_here), vis_here)
    enc_in[mine] = norm_rows(own_rows[...]).astype(BF16)
    gather_in = RingGather(sems, x, z_hi, functools.partial(own_block, enc_in), tp_device)
    gather_in.start()

    def slice_block(ring, pair, which, half=None):
        here = pl.ds(
            pl.multiple_of(seq_of(ring, pair, which) * slice_rows, slice_rows), slice_rows
        )
        if half is None:
            return w_p.at[:, here]
        return w_p.at[pl.ds(half * (N_TP // 2), N_TP // 2), here]

    def seq_device(ring, pair):
        return at_seq(seq_of(ring, pair, core))

    other_core = at_seq(seq_of(y, z_lo, 1 - core))
    gather_w = RingGather(
        sems, y, z_lo, lambda ring, pair, half: slice_block(ring, pair, core, half), seq_device
    )
    share_w = CoreShare(sems, slice_block, core, other_core)

    make_queries(4, 6)
    gather_in.partner()
    gather_in.sides()
    gather_in.partner_sides()
    got_p.wait()

    @pl.loop(1, N_TP)
    def _(d):
        remote(
            w_p_hbm.at[own_slice],
            w_p.at[(tp + N_TP - d) % N_TP, own_slice],
            slice_base + d,
            at_tp((tp + d) % N_TP),
        ).wait()

    gather_w.start()
    share_w.send(0, y, z_lo)
    got_in.wait()
    gather_in.far()
    gather_in.partner_far()

    @pl.loop(0, hidden.shape[1] // 256)
    def _(c):
        here = pl.ds(pl.multiple_of(c * 256, 256), 256)
        hidden[:, here] = jax.nn.gelu(dot(enc_in[...], w_in[:, here])).astype(BF16)

    gather_w.partner()
    share_w.send(1, y, 1 - z_lo)
    got_out.wait()
    part_base = sems.take(2 * N_TP)

    def part_rows(index):
        return pl.ds(pl.multiple_of(index * vis_here, vis_here), vis_here)

    def part_copy(h, d, source):
        to = (tp + d) % N_TP
        columns = pl.ds(h * half_width, half_width)
        return remote(
            part_out.at[part_rows(to), columns],
            part_in.at[source, :, columns],
            part_base + h * N_TP + d,
            at_tp(to),
        )

    for h in range(2):

        @pl.loop(0, half_width // 256)
        def _(c, h=h):
            here = pl.ds(pl.multiple_of(h * half_width + c * 256, 256), 256)
            part_out[:, here] = dot(hidden[...], w_out[:, here]).astype(BF16)

        @pl.loop(1, N_TP)
        def _(d, h=h):
            part_copy(h, d, tp).start()

    gather_w.sides()
    share_w.send(2, y + 3, z_lo)
    share_w.send(3, y + 1, z_lo)

    for h in range(2):
        columns = slice(h * half_width, (h + 1) * half_width)
        total = part_out[mine, columns].astype(F32)
        for d in range(1, N_TP):
            source = (tp + N_TP - d) % N_TP
            part_copy(h, d, source).wait()
            total = total + part_in[source, :, columns].astype(F32)
        own_rows[:, columns] = (own_rows[:, columns] + total).astype(BF16).astype(F32)

    key_in[mine] = norm_rows(own_rows[...]).astype(BF16)
    gather_key = RingGather(sems, x, z_hi, functools.partial(own_block, key_in), tp_device)
    gather_key.start()
    make_queries(6, 8)
    gather_key.partner()
    gather_key.sides()
    gather_key.partner_sides()
    gather_w.partner_sides()
    share_w.send(4, y + 3, 1 - z_lo)
    share_w.send(5, y + 1, 1 - z_lo)
    got_k.wait()
    got_v.wait()
    gather_key.far()
    gather_key.partner_far()

    kv_width = w_k.shape[1]
    own = seq_of(y, z_lo, core)
    kv[own, :, :kv_width] = dot(key_in[...], w_k[...]).astype(BF16)
    kv[own, :, kv_width:] = dot(key_in[...], w_v[...]).astype(BF16)

    def kv_block(ring, pair, which, half=None):
        index = seq_of(ring, pair, which)
        if half is None:
            return kv.at[index]
        return kv.at[index, pl.ds(half * (group // 2), group // 2)]

    gather_kv = RingGather(
        sems, y, z_lo, lambda ring, pair, half: kv_block(ring, pair, core, half), seq_device
    )
    share_kv = CoreShare(sems, kv_block, core, other_core)
    gather_kv.start()
    share_kv.send(0, y, z_lo)

    ones = jnp.ones((group, HEAD_DIM), BF16)

    def attend(here, blocks):
        for h in range(2):
            cols = slice(h * HEAD_DIM, (h + 1) * HEAD_DIM)
            v_cols = slice(kv_width + h * HEAD_DIM, kv_width + (h + 1) * HEAD_DIM)
            keys = jnp.concatenate([kv[b, :, cols] for b in blocks], axis=0)
            values = jnp.concatenate(
                [jnp.concatenate([kv[b, :, v_cols], ones], axis=1) for b in blocks], axis=0
            )
            scores = dot_t(q_ref[here, cols], keys)
            old = top_ref[h, here]
            new = jnp.maximum(old, jnp.max(scores, axis=1, keepdims=True))
            shrink = jnp.exp2(old - new)
            weights = jnp.exp2(scores - jnp.concatenate([new] * (2 * len(blocks)), axis=1))
            top_ref[h, here] = new
            acc_ref[h, here] = acc_ref[h, here] * jnp.concatenate([shrink] * 2, axis=1) + dot(
                weights.astype(BF16), values
            )

    top_ref[...] = jnp.full(top_ref.shape, -1e30, F32)
    acc_ref[...] = jnp.zeros(acc_ref.shape, F32)

    def both(ring, pair):
        return [seq_of(ring, pair, core), seq_of(ring, pair, 1 - core)]

    def attend_all(blocks):
        @pl.loop(0, rows // 256)
        def _(c):
            attend(pl.ds(pl.multiple_of(c * 256, 256), 256), blocks)

    gather_kv.partner()
    share_kv.send(1, y, 1 - z_lo)
    share_kv.wait(0, y, z_lo)
    share_kv.wait(1, y, 1 - z_lo)
    attend_all(both(y, z_lo) + both(y, 1 - z_lo))
    gather_kv.sides()
    share_kv.send(2, y + 3, z_lo)
    share_kv.send(3, y + 1, z_lo)
    gather_kv.partner_sides()
    share_kv.send(4, y + 3, 1 - z_lo)
    share_kv.send(5, y + 1, 1 - z_lo)
    gather_w.far()
    share_w.send(6, y + 2, z_lo)
    share_kv.wait(2, y + 3, z_lo)
    share_kv.wait(3, y + 1, z_lo)
    attend_all(both(y + 3, z_lo) + both(y + 1, z_lo))
    gather_kv.far()
    share_kv.send(6, y + 2, z_lo)
    gather_kv.partner_far()
    share_kv.send(7, y + 2, 1 - z_lo)
    share_kv.wait(4, y + 3, 1 - z_lo)
    share_kv.wait(5, y + 1, 1 - z_lo)
    attend_all(both(y + 3, 1 - z_lo) + both(y + 1, 1 - z_lo))
    gather_w.partner_far()
    share_w.send(7, y + 2, 1 - z_lo)
    share_kv.wait(6, y + 2, z_lo)
    share_kv.wait(7, y + 2, 1 - z_lo)

    att_base = sems.take(8)
    last_blocks = both(y + 2, z_lo) + both(y + 2, 1 - z_lo)

    def att_copy(i, b, to, source, of):
        return pltpu.make_async_remote_copy(
            src_ref=att_out.at[to],
            dst_ref=att_in.at[source],
            send_sem=send_sem.at[att_base + i * 2 + b],
            recv_sem=recv_sem.at[att_base + i * 2 + of],
            device_id=at_tp(to),
            device_id_type=MESH,
        )

    @pl.loop(0, 4)
    def _(i):
        ring = (x + 1 + i) % 4
        here = pl.ds(pl.multiple_of(ring * 256, 256), 256)
        attend(here, last_blocks)
        for h in range(2):
            done = acc_ref[h, here]
            done = (done[:, :HEAD_DIM] / done[:, HEAD_DIM:]).astype(BF16)
            cols = slice(h * HEAD_DIM, (h + 1) * HEAD_DIM)
            att_out[pl.ds(tp_of(ring, 0), 2), :, cols] = done.reshape(2, 128, HEAD_DIM)

        @pl.when(i < 3)
        def _():
            for b in range(2):
                att_copy(i, b, tp_of(ring, b), tp, z_hi).start()

    to_pair = tp_of(x, 1 - z_hi)
    att_copy(3, 0, to_pair, tp, 0).start()
    att_in[pl.ds(tp, 1)] = att_out[pl.ds(tp, 1)]

    for i, (ring, pair) in enumerate(
        ((y, z_lo), (y, 1 - z_lo), (y + 3, z_lo), (y + 1, z_lo))
        + ((y + 3, 1 - z_lo), (y + 1, 1 - z_lo), (y + 2, z_lo), (y + 2, 1 - z_lo))
    ):
        share_w.wait(i, ring, pair)

    @pl.loop(0, 3)
    def _(i):
        for b in range(2):
            to = tp_of(x + 1 + i, b)
            source = tp_of(x + 3 - i, b)
            copy = att_copy(i, b, to, source, b)
            copy.wait_send()
            copy.wait_recv()

    att_copy(3, 0, to_pair, to_pair, 0).wait()

    @pl.loop(0, width // 256)
    def _(c):
        here = pl.ds(pl.multiple_of(c * 256, 256), 256)
        total = dot(att_in[0], w_p[0, :, here])
        for t in range(1, N_TP):
            total = total + dot(att_in[t], w_p[t, :, here])
        proj[:, here] = total

    normal = norm_rows(proj[...])
    part = width // N_TP
    res_base = sems.take(N_TP)
    for t in range(N_TP):
        res_out[t] = normal[:, t * part : (t + 1) * part].astype(BF16)

    def res_copy(d, source):
        to = (tp + d) % N_TP
        return remote(res_out.at[to], out_ref.at[source], res_base + d, at_tp(to))

    @pl.loop(1, N_TP)
    def _(d):
        res_copy(d, tp).start()

    keep = pltpu.make_async_copy(res_out.at[tp], out_ref.at[tp], local_sem.at[7])
    keep.start()

    @pl.loop(1, N_TP)
    def _(d):
        res_copy(d, (tp + N_TP - d) % N_TP).wait()

    keep.wait()
    for transfer in (gather_in, gather_w, share_w, gather_key, gather_kv, share_kv):
        transfer.drain()


def shards(tokens, visible, w_in, w_out, w_query, w_key, w_value, w_proj):
    rows, width = tokens.shape
    tp_index = lax.axis_index("tp")
    part = width // N_TP
    vis_here = rows // 32
    group = vis_here * N_TP
    any_spec = pl.BlockSpec(memory_space=pl.ANY)
    vmem_spec = pl.BlockSpec(memory_space=pltpu.VMEM)
    heads = w_query.shape[1]
    visible = (visible > 0).astype(jnp.int32)
    result = pl.pallas_call(
        kernel,
        out_shape=jax.ShapeDtypeStruct((N_TP, rows // N_TP, part), BF16),
        in_specs=[vmem_spec] * 2 + [any_spec] * 7,
        out_specs=any_spec,
        scratch_shapes=[
            pltpu.VMEM(tokens.shape, BF16),
            pltpu.VMEM(w_in.shape, BF16),
            pltpu.VMEM(w_out.shape, BF16),
            pltpu.VMEM(w_query.shape, BF16),
            pltpu.VMEM(w_key.shape, BF16),
            pltpu.VMEM(w_value.shape, BF16),
            pltpu.VMEM((N_TP, *w_proj.shape), BF16),
            pltpu.VMEM((N_SEQ, 8, rows // 8), jnp.int32),
            pltpu.VMEM((16 * N_SEQ, width // 2), BF16),
            pltpu.VMEM((16 * N_SEQ, width // 2), BF16),
            pltpu.VMEM((vis_here, width), F32),
            pltpu.VMEM((group, width), BF16),
            pltpu.VMEM((group, w_in.shape[1]), BF16),
            pltpu.VMEM((group, width), BF16),
            pltpu.VMEM((N_TP, vis_here, width), BF16),
            pltpu.VMEM((group, width), BF16),
            pltpu.VMEM((N_SEQ, group, 2 * heads), BF16),
            pltpu.VMEM((rows, heads), BF16),
            pltpu.VMEM((2, rows, HEAD_DIM), F32),
            pltpu.VMEM((2, rows, 2 * HEAD_DIM), F32),
            pltpu.VMEM((N_TP, rows // N_TP, heads), BF16),
            pltpu.VMEM((N_TP, rows // N_TP, heads), BF16),
            pltpu.VMEM((rows // N_TP, width), F32),
            pltpu.VMEM((N_TP, rows // N_TP, part), BF16),
            pltpu.SemaphoreType.DMA((8,)),
            pltpu.SemaphoreType.DMA((136,)),
            pltpu.SemaphoreType.DMA((136,)),
        ],
        compiler_params=pltpu.CompilerParams(
            collective_id=0, has_side_effects=True, vmem_limit_bytes=60 * 1024 * 1024
        ),
        name="generator_step",
    )(
        visible.reshape(8, rows // 8),
        visible.reshape(1, rows),
        tokens,
        w_in,
        w_out,
        w_query,
        w_key,
        w_value,
        w_proj,
    )
    own_cols = lax.dynamic_slice_in_dim(tokens, tp_index * part, part, 1)
    return own_cols.astype(F32) + result.reshape(rows, part).astype(F32)


def solution(mesh):
    in_specs = (
        P("seq", None),
        P("seq"),
        P(None, "tp"),
        P("tp", None),
        P(None, "tp"),
        P(None, "tp"),
        P(None, "tp"),
        P("tp", None),
    )
    out_specs = P("seq", "tp")
    return jax.shard_map(shards, mesh=mesh, in_specs=in_specs, out_specs=out_specs, check_vma=False)
```

```python
import functools
import math

import jax
import jax.numpy as jnp
from jax import lax
from jax.experimental import pallas as pl
from jax.experimental.pallas import tpu as pltpu
from jax.sharding import PartitionSpec as P

HEAD_DIM = 128
EPSILON = 1e-05
MESH = pl.DeviceIdType.MESH
F32 = jnp.float32
BF16 = jnp.bfloat16
N_SEQ = 16
N_TP = 8


def norm_rows(values):
    row_mean = jnp.mean(values, axis=-1, keepdims=True)
    centred = values - row_mean
    variance = jnp.mean(centred * centred, axis=-1, keepdims=True)
    return centred * lax.rsqrt(variance + EPSILON)


def dot(a, b):
    return jnp.dot(a, b, preferred_element_type=F32)


def dot_t(a, b):
    return lax.dot_general(a, b, (((1,), (1,)), ((), ())), preferred_element_type=F32)


class Sems:
    def __init__(self, send, recv):
        self.send, self.recv, self.used = send, recv, 0

    def take(self, count):
        first = self.used
        self.used += count
        return first


class RingGather:
    def __init__(self, sems, ring, pair, block, device):
        self.sems, self.ring, self.pair = sems, ring, pair
        self.block, self.device = block, device
        self.base = sems.take(7)
        self.sent = []

    def _copy(self, i, ring, pair, device):
        ref = self.block(ring, pair)
        return pltpu.make_async_remote_copy(
            src_ref=ref,
            dst_ref=ref,
            send_sem=self.sems.send.at[self.base + i],
            recv_sem=self.sems.recv.at[self.base + i],
            device_id=device,
            device_id_type=MESH,
        )

    def _send(self, i, ring, pair, to_ring, to_pair):
        copy = self._copy(i, ring, pair, self.device(to_ring, to_pair))
        copy.start()
        self.sent.append(copy)

    def _wait(self, i, ring, pair):
        self._copy(i, ring, pair, self.device(self.ring, 1 - self.pair)).wait_recv()

    def start(self):
        r, p = self.ring, self.pair
        self._send(0, r, p, r, 1 - p)
        self._send(1, r, p, r + 1, p)
        self._send(2, r, p, r + 3, p)
        self._send(3, r, p, r + 2, p)

    def partner(self):
        r, p = self.ring, self.pair
        self._wait(0, r, 1 - p)
        self._send(4, r, 1 - p, r + 1, p)
        self._send(5, r, 1 - p, r + 3, p)

    def sides(self):
        self._wait(1, self.ring + 3, self.pair)
        self._wait(2, self.ring + 1, self.pair)

    def far(self):
        r, p = self.ring, self.pair
        self._wait(3, r + 2, p)
        self._send(6, r + 2, p, r, 1 - p)

    def partner_sides(self):
        self._wait(4, self.ring + 3, 1 - self.pair)
        self._wait(5, self.ring + 1, 1 - self.pair)

    def partner_far(self):
        self._wait(6, self.ring + 2, 1 - self.pair)

    def drain(self):
        for copy in self.sent:
            copy.wait_send()


class CoreShare:
    def __init__(self, sems, block, core, device):
        self.sems, self.block, self.core, self.device = sems, block, core, device
        self.base = sems.take(8)
        self.sent = []

    def _copy(self, i, ring, pair, core):
        ref = self.block(ring, pair, core)
        return pltpu.make_async_remote_copy(
            src_ref=ref,
            dst_ref=ref,
            send_sem=self.sems.send.at[self.base + i],
            recv_sem=self.sems.recv.at[self.base + i],
            device_id=self.device,
            device_id_type=MESH,
        )

    def send(self, i, ring, pair):
        copy = self._copy(i, ring, pair, self.core)
        copy.start()
        self.sent.append(copy)

    def wait(self, i, ring, pair):
        self._copy(i, ring, pair, 1 - self.core).wait_recv()

    def drain(self):
        for copy in self.sent:
            copy.wait_send()


def kernel(
    vis_tile,
    vis_row,
    tok_hbm,
    w_in_hbm,
    w_out_hbm,
    w_q_hbm,
    w_k_hbm,
    w_v_hbm,
    w_p_hbm,
    out_ref,
    tok,
    w_in,
    w_out,
    w_q,
    w_k,
    w_v,
    w_p,
    counts,
    pick_out,
    pick_in,
    own_rows,
    enc_in,
    hidden,
    part_out,
    far_in,
    both_out,
    side_in,
    pair_out,
    pair_in,
    key_in,
    kv,
    q_ref,
    top_ref,
    acc_ref,
    att_out,
    att_in,
    proj,
    res_out,
    local_sem,
    send_sem,
    recv_sem,
):
    rows, width = tok.shape
    seq = lax.axis_index("seq")
    tp = lax.axis_index("tp")
    core, z_lo, y = seq % 2, (seq // 2) % 2, seq // 4
    x, z_hi = tp // 2, tp % 2
    sems = Sems(send_sem, recv_sem)
    block_rows = own_rows.shape[0] // 2
    group = block_rows * N_TP
    half_width = width // 2

    def at_seq(index):
        return {"seq": index, "tp": tp}

    def at_tp(index):
        return {"seq": seq, "tp": index}

    def seq_of(ring, pair, which):
        return ((ring % 4) * 2 + pair) * 2 + which

    def tp_of(ring, pair):
        return (ring % 4) * 2 + pair

    slice_rows = w_p.shape[2] // 8

    def slice_of(ring, which):
        return pl.ds(pl.multiple_of(((ring % 4) * 2 + which) * slice_rows, slice_rows), slice_rows)

    own_slice = slice_of(y, core)
    loads = [
        pltpu.make_async_copy(src, dst, local_sem.at[i])
        for i, (src, dst) in enumerate(
            (
                (tok_hbm, tok),
                (w_p_hbm.at[own_slice], w_p.at[z_hi, x, own_slice]),
                (w_q_hbm, w_q),
                (w_in_hbm, w_in),
                (w_out_hbm, w_out),
                (w_k_hbm, w_k),
                (w_v_hbm, w_v),
            )
        )
    ]
    got_tok, got_p, got_q, got_in, got_out, got_k, got_v = loads
    for copy in loads[:2]:
        copy.start()

    barrier = pltpu.get_barrier_semaphore()

    @pl.loop(1, N_SEQ)
    def _(d):
        pl.semaphore_signal(
            barrier, inc=1, device_id=at_seq((seq + d) % N_SEQ), device_id_type=MESH
        )

    @pl.loop(1, N_TP)
    def _(d):
        pl.semaphore_signal(barrier, inc=1, device_id=at_tp((tp + d) % N_TP), device_id_type=MESH)

    visible = vis_row[...].astype(F32)
    lower = (
        lax.broadcasted_iota(jnp.int32, (rows, rows), 0)
        <= lax.broadcasted_iota(jnp.int32, (rows, rows), 1)
    ).astype(F32).astype(BF16)
    upto = dot(jnp.broadcast_to(visible, (8, rows)).astype(BF16), lower)[:1]

    pl.semaphore_wait(barrier, N_SEQ + N_TP - 2)

    def remote(src, dst, index, device):
        return pltpu.make_async_remote_copy(
            src_ref=src,
            dst_ref=dst,
            send_sem=send_sem.at[index],
            recv_sem=recv_sem.at[index],
            device_id=device,
            device_id_type=MESH,
        )

    count_base = sems.take(N_SEQ)

    @pl.loop(1, N_SEQ)
    def _(d):
        remote(
            vis_tile, counts.at[seq], count_base + d, at_seq((seq + d) % N_SEQ)
        ).start()

    counts[pl.ds(seq, 1)] = vis_tile[...][None]

    slice_base = sems.take(8)
    pair_device = at_tp(tp_of(x, 1 - z_hi))
    remote(
        w_p_hbm.at[own_slice], w_p.at[z_hi, x, own_slice], slice_base, pair_device
    ).start()

    def slice_copy(of, d, ring):
        here = w_p.at[of, ring, own_slice]
        src = w_p_hbm.at[own_slice] if of is z_hi else w_p.at[of, x, own_slice]
        index = slice_base + d + (0 if of is z_hi else 4)
        return remote(src, here, index, at_tp(tp_of(x + d, z_hi)))

    @pl.loop(1, 4)
    def _(d):
        slice_copy(z_hi, d, x).start()

    @pl.loop(1, N_SEQ)
    def _(d):
        remote(
            vis_tile, counts.at[(seq + N_SEQ - d) % N_SEQ], count_base + d, at_seq((seq + d) % N_SEQ)
        ).wait()

    lane_source = lax.broadcasted_iota(jnp.int32, (1, 256), 1) // 16
    before_me = jnp.zeros((1, 1), F32)
    lane_before = jnp.zeros((1, 256), F32)
    lane_count = jnp.zeros((1, 256), F32)
    for s in range(N_SEQ):
        count = jnp.sum(counts[s].astype(F32), axis=1, keepdims=True)
        count = jnp.sum(count, axis=0, keepdims=True)
        before_me = before_me + jnp.where(seq > s, 1.0, 0.0) * count
        lane_before = lane_before + jnp.where(lane_source > s, count, 0.0)
        lane_count = lane_count + jnp.where(lane_source == s, count, 0.0)

    rank = (before_me + upto - 1.0).astype(jnp.int32)
    code = ((rank >> 3) & 15) * 8 + ((rank >> 7) & 7)
    code = jnp.where((visible > 0.0) & ((rank & 7) == tp), code, -1)
    picks = (lax.broadcasted_iota(jnp.int32, (128, rows), 0) == code).astype(F32).astype(BF16)
    got_tok.wait()
    for h in range(2):
        for c in range(0, half_width, 640):
            rows_of = dot(picks, tok[:, h * half_width + c : h * half_width + c + 640])
            rows_of = rows_of.reshape(16, 8, 640)
            if h == 0:
                proj[:, c : c + 640] = rows_of.reshape(128, 640)
            else:
                first = proj[:, c : c + 640].reshape(16, 8, 640)
                both = jnp.concatenate([first, rows_of], axis=1)
                pick_out[:, c : c + 640] = both.reshape(256, 640).astype(BF16)

    pick_base = sems.take(N_SEQ)

    def pick_rows(index):
        return pl.ds(pl.multiple_of(index * 16, 16), 16)

    @pl.loop(1, N_SEQ)
    def _(d):
        to = (seq + d) % N_SEQ
        remote(
            pick_out.at[pick_rows(to)], pick_in.at[pick_rows(seq)], pick_base + d, at_seq(to)
        ).start()

    pick_in[pick_rows(seq)] = pick_out[pick_rows(seq)]
    other_z = 1 - z_hi
    remote(
        w_p_hbm.at[own_slice], w_p.at[other_z, x, own_slice], slice_base, pair_device
    ).wait()

    @pl.loop(1, 4)
    def _(d):
        slice_copy(other_z, d, x).start()

    for copy in loads[2:]:
        copy.start()

    query_scale = HEAD_DIM ** (-0.5) * math.log2(math.e)
    got_q.wait()

    def make_queries(first, last):
        @pl.loop(first, last)
        def _(c):
            here = pl.ds(pl.multiple_of(c * 128, 128), 128)
            normed = norm_rows(tok[here].astype(F32)).astype(BF16)
            q_ref[here] = (dot(normed, w_q[...]) * query_scale).astype(BF16)

    make_queries(0, 4)

    @pl.loop(1, N_SEQ)
    def _(d):
        to = (seq + d) % N_SEQ
        source = (seq + N_SEQ - d) % N_SEQ
        remote(
            pick_out.at[pick_rows(to)], pick_in.at[pick_rows(source)], pick_base + d, at_seq(to)
        ).wait()

    slot = lax.broadcasted_iota(jnp.int32, (2 * block_rows, 256), 0)
    lane = lax.broadcasted_iota(jnp.int32, (2 * block_rows, 256), 1)
    wanted = (slot * 128 + seq * 8 + tp).astype(F32)
    live = (wanted >= lane_before) & (wanted < lane_before + lane_count)
    live = live & ((lane & 7) == (slot & 7))
    for h in range(2):
        chosen = (live & (((lane >> 3) & 1) == h)).astype(F32).astype(BF16)
        own_rows[:, h * half_width : (h + 1) * half_width] = dot(chosen, pick_in[...])

    def own_block(ref, a, ring, pair):
        first = tp_of(ring, pair) * block_rows
        return ref.at[a, pl.ds(pl.multiple_of(first, block_rows), block_rows)]

    def tp_device(ring, pair):
        return at_tp(tp_of(ring, pair))

    mine = pl.ds(pl.multiple_of(tp * block_rows, block_rows), block_rows)
    halves = [slice(a * block_rows, (a + 1) * block_rows) for a in range(2)]
    gather_in = []
    for a in range(2):
        enc_in[a, mine] = norm_rows(own_rows[halves[a]]).astype(BF16)
        gather_in.append(
            RingGather(sems, x, z_hi, functools.partial(own_block, enc_in, a), tp_device)
        )
        gather_in[a].start()

    def w_block(ring, which, half=None):
        if half is None:
            return w_p.at[:, :, slice_of(ring, which)]
        return w_p.at[half, :, slice_of(ring, which)]

    def seq_device(ring, pair):
        return at_seq(seq_of(ring, pair, core))

    other_core = at_seq(seq_of(y, z_lo, 1 - core))
    up, down = seq_device(y + 1, z_lo), seq_device(y + 3, z_lo)
    w_base = sems.take(8)

    def w_copy(i, ring, which=None, half=None):
        ref = w_block(ring, core if which is None else which, half)
        return remote(ref, ref, w_base + i, (up, down, up, down)[i] if i < 4 else other_core)

    def w_start():
        got_p.wait()

        @pl.loop(1, 4)
        def _(d):
            slice_copy(z_hi, d, (x + 4 - d) % 4).wait()

        @pl.loop(1, 4)
        def _(d):
            slice_copy(other_z, d, (x + 4 - d) % 4).wait()

        w_copy(0, y).start()
        w_copy(1, y).start()
        w_copy(4, y).start()

    def w_sides():
        w_copy(0, y + 3).wait_recv()
        w_copy(2, y + 3, half=0).start()
        w_copy(5, y + 3).start()
        w_copy(1, y + 1).wait_recv()
        w_copy(3, y + 1, half=1).start()
        w_copy(6, y + 1).start()

    def w_far():
        w_copy(2, y + 2, half=0).wait_recv()
        w_copy(3, y + 2, half=1).wait_recv()
        w_copy(7, y + 2).start()
        for i, ring in enumerate((y, y + 3, y + 1, y + 2)):
            w_copy(4 + i, ring, 1 - core).wait_recv()

    def w_drain():
        for i, ring in enumerate((y, y, y + 3, y + 1, y, y + 3, y + 1, y + 2)):
            w_copy(i, ring, half=(None, None, 0, 1)[i] if i < 4 else None).wait_send()

    def to_hidden(a):
        @pl.loop(0, hidden.shape[2] // 256)
        def _(c):
            here = pl.ds(pl.multiple_of(c * 256, 256), 256)
            hidden[a, :, here] = jax.nn.gelu(dot(enc_in[a], w_in[:, here])).astype(BF16)

    def to_part(a):
        @pl.loop(0, width // 256)
        def _(c):
            here = pl.ds(pl.multiple_of(c * 256, 256), 256)
            part_out[a, :, here] = dot(hidden[a], w_out[:, here]).astype(BF16)

    slab_rows = 2 * block_rows
    low, high = pl.ds(0, half_width), pl.ds(half_width, half_width)
    sum_base = [sems.take(7), sems.take(7)]
    right, left = at_tp(tp_of(x + 1, z_hi)), at_tp(tp_of(x + 3, z_hi))

    def slab(ring):
        return pl.ds(pl.multiple_of((ring % 4) * slab_rows, slab_rows), slab_rows)

    def of_pair(pair):
        return pl.ds(pl.multiple_of(pair * block_rows, block_rows), block_rows)

    def of_both(pair):
        first = (x * 2 + pair) * block_rows
        return pl.ds(pl.multiple_of(first, block_rows), block_rows)

    def sum_copy(a, i):
        part, side = part_out.at[a], side_in.at[a]
        src, dst, to = (
            lambda: (part.at[slab(x + 2), low], far_in.at[a, 0], right),
            lambda: (part.at[slab(x + 2), high], far_in.at[a, 1], left),
            lambda: (part.at[slab(x + 1), high], side.at[0, :, high], right),
            lambda: (part.at[slab(x + 3), low], side.at[1, :, low], left),
            lambda: (both_out.at[a, 0], side.at[0, :, low], right),
            lambda: (both_out.at[a, 1], side.at[1, :, high], left),
            lambda: (pair_out.at[a], pair_in.at[a], at_tp(tp_of(x, 1 - z_hi))),
        )[i]()
        return remote(src, dst, sum_base[a] + i, to)

    def sum_start(a):
        for i in range(4):
            sum_copy(a, i).start()

    def sum_add(a):
        for i, (ring, columns) in enumerate(((x + 1, low), (x + 3, high))):
            sum_copy(a, i).wait_recv()
            own = part_out[a, slab(ring), columns].astype(F32)
            both_out[a, i] = (own + far_in[a, i].astype(F32)).astype(BF16)
            sum_copy(a, 4 + i).start()

    def sum_of_pair(a, pair):
        total = part_out[a, of_both(pair)].astype(F32)
        return total + sum(side_in[a, i, of_pair(pair)].astype(F32) for i in range(2))

    def sum_swap(a):
        for i in range(2, 6):
            sum_copy(a, i).wait_recv()
        pair_out[a] = sum_of_pair(a, 1 - z_hi).astype(BF16)
        sum_copy(a, 6).start()

    gather_key = [
        RingGather(sems, x, z_hi, functools.partial(own_block, key_in, a), tp_device)
        for a in range(2)
    ]

    def sum_end(a):
        total = own_rows[halves[a]] + sum_of_pair(a, z_hi)
        sum_copy(a, 6).wait_recv()
        encoded = (total + pair_in[a].astype(F32)).astype(BF16).astype(F32)
        key_in[a, mine] = norm_rows(encoded).astype(BF16)
        gather_key[a].start()

    kv_width = w_k.shape[1]
    own = seq_of(y, z_lo, core)

    def kv_block(a, ring, pair, which):
        return kv.at[seq_of(ring, pair, which), a]

    def kv_gather(a):
        return RingGather(
            sems, y, z_lo, lambda ring, pair: kv_block(a, ring, pair, core), seq_device
        )

    gather_kv = [kv_gather(a) for a in range(2)]
    share_kv = [
        CoreShare(sems, functools.partial(kv_block, a), core, other_core) for a in range(2)
    ]

    def to_kv(a):
        kv[own, a, :, :kv_width] = dot(key_in[a], w_k[...]).astype(BF16)
        kv[own, a, :, kv_width:] = dot(key_in[a], w_v[...]).astype(BF16)
        gather_kv[a].start()
        share_kv[a].send(0, y, z_lo)

    def kv_partner(a):
        gather_kv[a].partner()
        share_kv[a].send(1, y, 1 - z_lo)

    def kv_sides(a):
        gather_kv[a].sides()
        share_kv[a].send(2, y + 3, z_lo)
        share_kv[a].send(3, y + 1, z_lo)

    def kv_partner_sides(a):
        gather_kv[a].partner_sides()
        share_kv[a].send(4, y + 3, 1 - z_lo)
        share_kv[a].send(5, y + 1, 1 - z_lo)

    def kv_far(a):
        gather_kv[a].far()
        share_kv[a].send(6, y + 2, z_lo)

    def kv_partner_far(a):
        gather_kv[a].partner_far()
        share_kv[a].send(7, y + 2, 1 - z_lo)

    ones = jnp.ones((group, HEAD_DIM), BF16)

    def attend(here, a, blocks):
        for h in range(2):
            cols = slice(h * HEAD_DIM, (h + 1) * HEAD_DIM)
            v_cols = slice(kv_width + h * HEAD_DIM, kv_width + (h + 1) * HEAD_DIM)
            keys = jnp.concatenate([kv[b, a, :, cols] for b in blocks], axis=0)
            values = jnp.concatenate(
                [jnp.concatenate([kv[b, a, :, v_cols], ones], axis=1) for b in blocks], axis=0
            )
            scores = dot_t(q_ref[here, cols], keys)
            old = top_ref[h, here]
            new = jnp.maximum(old, jnp.max(scores, axis=1, keepdims=True))
            shrink = jnp.exp2(old - new)
            spread = jnp.concatenate([new] * (scores.shape[1] // HEAD_DIM), axis=1)
            weights = jnp.exp2(scores - spread)
            top_ref[h, here] = new
            acc_ref[h, here] = acc_ref[h, here] * jnp.concatenate([shrink] * 2, axis=1) + dot(
                weights.astype(BF16), values
            )

    pairs = (
        ((y, z_lo), (y, 1 - z_lo)),
        ((y + 3, z_lo), (y + 1, z_lo)),
        ((y + 3, 1 - z_lo), (y + 1, 1 - z_lo)),
        ((y + 2, z_lo), (y + 2, 1 - z_lo)),
    )

    def blocks_of(step):
        places = pairs[2 * step] + pairs[2 * step + 1]
        return [seq_of(*place, c) for place in places for c in (core, 1 - core)]

    def share_wait(a, step):
        for i in range(4):
            share_kv[a].wait(4 * step + i, *pairs[2 * step + i // 2][i % 2])

    def attend_all(a, step):
        share_wait(a, step)
        blocks = blocks_of(step)

        @pl.loop(0, rows // 512)
        def _(c):
            attend(pl.ds(pl.multiple_of(c * 512, 512), 512), a, blocks)

    make_queries(4, 6)
    w_start()
    gather_in[0].partner()
    gather_in[0].sides()
    gather_in[0].far()
    gather_in[1].partner()
    gather_in[1].sides()
    gather_in[1].far()
    gather_in[0].partner_sides()
    got_in.wait()
    gather_in[0].partner_far()
    to_hidden(0)
    got_out.wait()
    to_part(0)
    sum_start(0)
    gather_in[1].partner_sides()
    gather_in[1].partner_far()
    to_hidden(1)
    to_part(1)
    sum_add(0)
    sum_start(1)
    sum_swap(0)
    sum_add(1)
    sum_end(0)
    sum_swap(1)
    make_queries(6, 8)
    gather_key[0].partner()
    gather_key[0].sides()
    gather_key[0].far()
    sum_end(1)
    gather_key[0].partner_sides()
    got_k.wait()
    got_v.wait()
    gather_key[0].partner_far()
    to_kv(0)
    gather_key[1].partner()
    gather_key[1].sides()
    gather_key[1].far()
    kv_partner(0)
    kv_sides(0)
    kv_far(0)
    gather_key[1].partner_sides()
    gather_key[1].partner_far()
    to_kv(1)
    top_ref[...] = jnp.full(top_ref.shape, -1e30, F32)
    acc_ref[...] = jnp.zeros(acc_ref.shape, F32)
    kv_partner_sides(0)
    kv_partner_far(0)
    attend_all(0, 0)
    kv_partner(1)
    kv_sides(1)
    kv_far(1)
    w_sides()
    attend_all(0, 1)
    kv_partner_sides(1)
    kv_partner_far(1)
    attend_all(1, 0)
    share_wait(1, 1)

    att_base = sems.take(8)
    last_blocks = blocks_of(1)

    def att_copy(i, b, to, source, of):
        return pltpu.make_async_remote_copy(
            src_ref=att_out.at[to],
            dst_ref=att_in.at[source],
            send_sem=send_sem.at[att_base + i * 2 + b],
            recv_sem=recv_sem.at[att_base + i * 2 + of],
            device_id=at_tp(to),
            device_id_type=MESH,
        )

    @pl.loop(0, 4)
    def _(i):
        ring = (x + 1 + i) % 4
        here = pl.ds(pl.multiple_of(ring * 256, 256), 256)
        attend(here, 1, last_blocks)
        for h in range(2):
            done = acc_ref[h, here]
            done = (done[:, :HEAD_DIM] / done[:, HEAD_DIM:]).astype(BF16)
            cols = slice(h * HEAD_DIM, (h + 1) * HEAD_DIM)
            att_out[pl.ds(tp_of(ring, 0), 2), :, cols] = done.reshape(2, 128, HEAD_DIM)

        @pl.when(i < 3)
        def _():
            for b in range(2):
                att_copy(i, b, tp_of(ring, b), tp, z_hi).start()

    to_pair = tp_of(x, 1 - z_hi)
    att_copy(3, 0, to_pair, tp, 0).start()
    att_in[pl.ds(tp, 1)] = att_out[pl.ds(tp, 1)]

    w_far()

    @pl.loop(0, 3)
    def _(i):
        for b in range(2):
            to = tp_of(x + 1 + i, b)
            source = tp_of(x + 3 - i, b)
            copy = att_copy(i, b, to, source, b)
            copy.wait_send()
            copy.wait_recv()

    att_copy(3, 0, to_pair, to_pair, 0).wait()

    @pl.loop(0, width // 256)
    def _(c):
        here = pl.ds(pl.multiple_of(c * 256, 256), 256)
        total = dot(att_in[0], w_p[0, 0, :, here])
        for t in range(1, N_TP):
            total = total + dot(att_in[t], w_p[t % 2, t // 2, :, here])
        proj[:, here] = total

    normal = norm_rows(proj[...])
    part = width // N_TP
    res_base = sems.take(N_TP)
    for t in range(N_TP):
        columns = normal[:, t * part : (t + 1) * part]
        half_rows = columns.shape[0] // 2
        sides = jnp.concatenate([columns[:half_rows], columns[half_rows:]], axis=1)
        res_out[t] = sides.astype(BF16)

    def res_copy(d, source):
        to = (tp + d) % N_TP
        return remote(res_out.at[to], out_ref.at[source], res_base + d, at_tp(to))

    @pl.loop(1, N_TP)
    def _(d):
        res_copy(d, tp).start()

    keep = pltpu.make_async_copy(res_out.at[tp], out_ref.at[tp], local_sem.at[7])
    keep.start()

    @pl.loop(1, N_TP)
    def _(d):
        res_copy(d, (tp + N_TP - d) % N_TP).wait()

    keep.wait()
    assert sems.used <= 160
    for transfer in (*gather_in, *gather_key, *gather_kv, *share_kv):
        transfer.drain()
    for a in range(2):
        for i in range(7):
            sum_copy(a, i).wait_send()
    w_drain()


def add_kernel(tok_ref, normal_ref, out_ref):
    rows, part = out_ref.shape
    which = lax.axis_index("tp") % 2
    own = jnp.where(which == 0, tok_ref[:, :part].astype(F32), tok_ref[:, part:].astype(F32))
    normal = normal_ref[...].astype(F32)
    normal = jnp.concatenate([normal[:, :, :part], normal[:, :, part:]], axis=1)
    out_ref[...] = own + normal.reshape(rows, part)


def shards(tokens, visible, w_in, w_out, w_query, w_key, w_value, w_proj):
    rows, width = tokens.shape
    part = width // N_TP
    block_rows = rows // 64
    group = block_rows * N_TP
    any_spec = pl.BlockSpec(memory_space=pl.ANY)
    vmem_spec = pl.BlockSpec(memory_space=pltpu.VMEM)
    heads = w_query.shape[1]
    result = pl.pallas_call(
        kernel,
        out_shape=jax.ShapeDtypeStruct((N_TP, rows // N_TP // 2, 2 * part), BF16),
        in_specs=[vmem_spec] * 2 + [any_spec] * 7,
        out_specs=any_spec,
        scratch_shapes=[
            pltpu.VMEM(tokens.shape, BF16),
            pltpu.VMEM(w_in.shape, BF16),
            pltpu.VMEM(w_out.shape, BF16),
            pltpu.VMEM(w_query.shape, BF16),
            pltpu.VMEM(w_key.shape, BF16),
            pltpu.VMEM(w_value.shape, BF16),
            pltpu.VMEM((2, 4, *w_proj.shape), BF16),
            pltpu.VMEM((N_SEQ, 8, rows // 8), jnp.int32),
            pltpu.VMEM((16 * N_SEQ, width // 2), BF16),
            pltpu.VMEM((16 * N_SEQ, width // 2), BF16),
            pltpu.VMEM((2 * block_rows, width), F32),
            pltpu.VMEM((2, group, width), BF16),
            pltpu.VMEM((2, group, w_in.shape[1]), BF16),
            pltpu.VMEM((2, group, width), BF16),
            pltpu.VMEM((2, 2, 2 * block_rows, width // 2), BF16),
            pltpu.VMEM((2, 2, 2 * block_rows, width // 2), BF16),
            pltpu.VMEM((2, 2, 2 * block_rows, width), BF16),
            pltpu.VMEM((2, block_rows, width), BF16),
            pltpu.VMEM((2, block_rows, width), BF16),
            pltpu.VMEM((2, group, width), BF16),
            pltpu.VMEM((N_SEQ, 2, group, 2 * heads), BF16),
            pltpu.VMEM((rows, heads), BF16),
            pltpu.VMEM((2, rows, HEAD_DIM), F32),
            pltpu.VMEM((2, rows, 2 * HEAD_DIM), F32),
            pltpu.VMEM((N_TP, rows // N_TP, heads), BF16),
            pltpu.VMEM((N_TP, rows // N_TP, heads), BF16),
            pltpu.VMEM((rows // N_TP, width), F32),
            pltpu.VMEM((N_TP, rows // N_TP // 2, 2 * part), BF16),
            pltpu.SemaphoreType.DMA((8,)),
            pltpu.SemaphoreType.DMA((160,)),
            pltpu.SemaphoreType.DMA((160,)),
        ],
        compiler_params=pltpu.CompilerParams(
            collective_id=0, has_side_effects=True, vmem_limit_bytes=60 * 1024 * 1024
        ),
        name="generator_step",
    )(
        visible.reshape(8, rows // 8),
        visible.reshape(1, rows),
        tokens,
        w_in,
        w_out,
        w_query,
        w_key,
        w_value,
        w_proj,
    )
    tile = rows // 4
    return pl.pallas_call(
        add_kernel,
        grid=(rows // tile,),
        out_shape=jax.ShapeDtypeStruct((rows, part), F32),
        in_specs=[
            pl.BlockSpec((tile, 2 * part), lambda i: (i, lax.axis_index("tp") // 2)),
            pl.BlockSpec((N_TP // 4, rows // N_TP // 2, 2 * part), lambda i: (i, 0, 0)),
        ],
        out_specs=pl.BlockSpec((tile, part), lambda i: (i, 0)),
        name="residual",
    )(tokens, result)


def solution(mesh):
    in_specs = (
        P("seq", None),
        P("seq"),
        P(None, "tp"),
        P("tp", None),
        P(None, "tp"),
        P(None, "tp"),
        P(None, "tp"),
        P("tp", None),
    )
    out_specs = P("seq", "tp")
    return jax.shard_map(shards, mesh=mesh, in_specs=in_specs, out_specs=out_specs, check_vma=False)
```

```python
import functools
import math

import jax
import jax.numpy as jnp
from jax import lax
from jax.experimental import pallas as pl
from jax.experimental.pallas import tpu as pltpu
from jax.sharding import PartitionSpec as P

HEAD_DIM = 128
EPSILON = 1e-05
MESH = pl.DeviceIdType.MESH
F32 = jnp.float32
BF16 = jnp.bfloat16
N_SEQ = 16
N_TP = 8


def norm_rows(values):
    row_mean = jnp.mean(values, axis=-1, keepdims=True)
    centred = values - row_mean
    variance = jnp.mean(centred * centred, axis=-1, keepdims=True)
    return centred * lax.rsqrt(variance + EPSILON)


def dot(a, b):
    return jnp.dot(a, b, preferred_element_type=F32)


def dot_t(a, b):
    return lax.dot_general(a, b, (((1,), (1,)), ((), ())), preferred_element_type=F32)


class Sems:
    def __init__(self, send, recv):
        self.send, self.recv, self.used = send, recv, 0

    def take(self, count):
        first = self.used
        self.used += count
        return first


class RingGather:
    def __init__(self, sems, ring, pair, block, device, half=None):
        self.sems, self.ring, self.pair, self.half = sems, ring, pair, half
        self.block, self.device = block, device
        self.base = sems.take(8)
        self.sent = []

    def _copy(self, i, ring, pair, device):
        ref = self.block(ring, pair)
        if self.half is not None and i in (3, 7):
            ref = self.half(ref, i // 7)
        return pltpu.make_async_remote_copy(
            src_ref=ref,
            dst_ref=ref,
            send_sem=self.sems.send.at[self.base + i],
            recv_sem=self.sems.recv.at[self.base + i],
            device_id=device,
            device_id_type=MESH,
        )

    def _send(self, i, ring, pair, to_ring, to_pair):
        copy = self._copy(i, ring, pair, self.device(to_ring, to_pair))
        copy.start()
        self.sent.append(copy)

    def _wait(self, i, ring, pair):
        self._copy(i, ring, pair, self.device(self.ring, 1 - self.pair)).wait_recv()

    def start(self):
        r, p = self.ring, self.pair
        self._send(0, r, p, r, 1 - p)
        self._send(1, r, p, r + 1, p)
        self._send(2, r, p, r + 3, p)
        if self.half is None:
            self._send(3, r, p, r + 2, p)

    def partner(self):
        r, p = self.ring, self.pair
        self._wait(0, r, 1 - p)
        self._send(4, r, 1 - p, r + 1, p)
        self._send(5, r, 1 - p, r + 3, p)

    def sides(self):
        r, p = self.ring, self.pair
        self._wait(1, r + 3, p)
        if self.half is not None:
            self._send(3, r + 3, p, r + 1, p)
        self._wait(2, r + 1, p)
        if self.half is not None:
            self._send(7, r + 1, p, r + 3, p)

    def far(self):
        r, p = self.ring, self.pair
        self._wait(3, r + 2, p)
        if self.half is not None:
            self._wait(7, r + 2, p)
        self._send(6, r + 2, p, r, 1 - p)

    def partner_sides(self):
        self._wait(4, self.ring + 3, 1 - self.pair)
        self._wait(5, self.ring + 1, 1 - self.pair)

    def partner_far(self):
        self._wait(6, self.ring + 2, 1 - self.pair)

    def drain(self):
        for copy in self.sent:
            copy.wait_send()


class CoreShare:
    def __init__(self, sems, block, core, device):
        self.sems, self.block, self.core, self.device = sems, block, core, device
        self.base = sems.take(8)
        self.sent = []

    def _copy(self, i, ring, pair, core):
        ref = self.block(ring, pair, core)
        return pltpu.make_async_remote_copy(
            src_ref=ref,
            dst_ref=ref,
            send_sem=self.sems.send.at[self.base + i],
            recv_sem=self.sems.recv.at[self.base + i],
            device_id=self.device,
            device_id_type=MESH,
        )

    def send(self, i, ring, pair):
        copy = self._copy(i, ring, pair, self.core)
        copy.start()
        self.sent.append(copy)

    def wait(self, i, ring, pair):
        self._copy(i, ring, pair, 1 - self.core).wait_recv()

    def drain(self):
        for copy in self.sent:
            copy.wait_send()


def kernel(
    vis_tile,
    vis_row,
    tok_hbm,
    w_in_hbm,
    w_out_hbm,
    w_q_hbm,
    w_k_hbm,
    w_v_hbm,
    w_p_hbm,
    out_ref,
    tok,
    w_in,
    w_out,
    w_q,
    w_k,
    w_v,
    w_p,
    counts,
    pick_out,
    pick_in,
    own_rows,
    enc_in,
    hidden,
    part_out,
    far_in,
    both_out,
    side_in,
    pair_out,
    pair_in,
    key_in,
    kv,
    q_ref,
    top_ref,
    acc_ref,
    att_out,
    att_in,
    proj,
    res_out,
    res_in,
    stat_out,
    stat_in,
    own_cols,
    result,
    local_sem,
    send_sem,
    recv_sem,
):
    rows, width = tok.shape
    seq = lax.axis_index("seq")
    tp = lax.axis_index("tp")
    core, z_lo, y = seq % 2, (seq // 2) % 2, seq // 4
    x, z_hi = tp // 2, tp % 2
    sems = Sems(send_sem, recv_sem)
    block_rows = own_rows.shape[0] // 2
    group = block_rows * N_TP
    half_width = width // 2

    def at_seq(index):
        return {"seq": index, "tp": tp}

    def at_tp(index):
        return {"seq": seq, "tp": index}

    def seq_of(ring, pair, which):
        return ((ring % 4) * 2 + pair) * 2 + which

    def tp_of(ring, pair):
        return (ring % 4) * 2 + pair

    slice_rows = w_p.shape[2] // 8

    def slice_of(ring, which):
        return pl.ds(pl.multiple_of(((ring % 4) * 2 + which) * slice_rows, slice_rows), slice_rows)

    own_slice = slice_of(y, core)
    loads = [
        pltpu.make_async_copy(src, dst, local_sem.at[i])
        for i, (src, dst) in enumerate(
            (
                (tok_hbm, tok),
                (w_p_hbm.at[own_slice], w_p.at[z_hi, x, own_slice]),
                (w_q_hbm, w_q),
                (w_in_hbm, w_in),
                (w_out_hbm, w_out),
                (w_k_hbm, w_k),
                (w_v_hbm, w_v),
            )
        )
    ]
    got_tok, got_p, got_q, got_in, got_out, got_k, got_v = loads
    for copy in loads[:2]:
        copy.start()

    barrier = pltpu.get_barrier_semaphore()

    @pl.loop(1, N_SEQ)
    def _(d):
        pl.semaphore_signal(
            barrier, inc=1, device_id=at_seq((seq + d) % N_SEQ), device_id_type=MESH
        )

    @pl.loop(1, N_TP)
    def _(d):
        pl.semaphore_signal(barrier, inc=1, device_id=at_tp((tp + d) % N_TP), device_id_type=MESH)

    visible = vis_row[...].astype(F32)
    lower = (
        lax.broadcasted_iota(jnp.int32, (rows, rows), 0)
        <= lax.broadcasted_iota(jnp.int32, (rows, rows), 1)
    ).astype(F32).astype(BF16)
    upto = dot(jnp.broadcast_to(visible, (8, rows)).astype(BF16), lower)[:1]

    pl.semaphore_wait(barrier, N_SEQ + N_TP - 2)

    def remote(src, dst, index, device):
        return pltpu.make_async_remote_copy(
            src_ref=src,
            dst_ref=dst,
            send_sem=send_sem.at[index],
            recv_sem=recv_sem.at[index],
            device_id=device,
            device_id_type=MESH,
        )

    count_base = sems.take(N_SEQ)

    @pl.loop(1, N_SEQ)
    def _(d):
        remote(
            vis_tile, counts.at[seq], count_base + d, at_seq((seq + d) % N_SEQ)
        ).start()

    counts[pl.ds(seq, 1)] = vis_tile[...][None]

    slice_base = sems.take(8)
    pair_device = at_tp(tp_of(x, 1 - z_hi))
    remote(
        w_p_hbm.at[own_slice], w_p.at[z_hi, x, own_slice], slice_base, pair_device
    ).start()

    def slice_copy(of, d, ring):
        here = w_p.at[of, ring, own_slice]
        src = w_p_hbm.at[own_slice] if of is z_hi else w_p.at[of, x, own_slice]
        index = slice_base + d + (0 if of is z_hi else 4)
        return remote(src, here, index, at_tp(tp_of(x + d, z_hi)))

    @pl.loop(1, 4)
    def _(d):
        slice_copy(z_hi, d, x).start()

    @pl.loop(1, N_SEQ)
    def _(d):
        remote(
            vis_tile, counts.at[(seq + N_SEQ - d) % N_SEQ], count_base + d, at_seq((seq + d) % N_SEQ)
        ).wait()

    lane_source = lax.broadcasted_iota(jnp.int32, (1, 256), 1) // 16
    before_me = jnp.zeros((1, 1), F32)
    lane_before = jnp.zeros((1, 256), F32)
    lane_count = jnp.zeros((1, 256), F32)
    for s in range(N_SEQ):
        count = jnp.sum(counts[s].astype(F32), axis=1, keepdims=True)
        count = jnp.sum(count, axis=0, keepdims=True)
        before_me = before_me + jnp.where(seq > s, 1.0, 0.0) * count
        lane_before = lane_before + jnp.where(lane_source > s, count, 0.0)
        lane_count = lane_count + jnp.where(lane_source == s, count, 0.0)

    rank = (before_me + upto - 1.0).astype(jnp.int32)
    code = ((rank >> 3) & 15) * 8 + ((rank >> 7) & 7)
    code = jnp.where((visible > 0.0) & ((rank & 7) == tp), code, -1)
    picks = (lax.broadcasted_iota(jnp.int32, (128, rows), 0) == code).astype(F32).astype(BF16)
    got_tok.wait()
    for h in range(2):
        for c in range(0, half_width, 640):
            rows_of = dot(picks, tok[:, h * half_width + c : h * half_width + c + 640])
            rows_of = rows_of.reshape(16, 8, 640)
            if h == 0:
                proj[:, c : c + 640] = rows_of.reshape(128, 640)
            else:
                first = proj[:, c : c + 640].reshape(16, 8, 640)
                both = jnp.concatenate([first, rows_of], axis=1)
                pick_out[:, c : c + 640] = both.reshape(256, 640).astype(BF16)

    pick_base = sems.take(N_SEQ)

    def pick_rows(index):
        return pl.ds(pl.multiple_of(index * 16, 16), 16)

    @pl.loop(1, N_SEQ)
    def _(d):
        to = (seq + d) % N_SEQ
        remote(
            pick_out.at[pick_rows(to)], pick_in.at[pick_rows(seq)], pick_base + d, at_seq(to)
        ).start()

    pick_in[pick_rows(seq)] = pick_out[pick_rows(seq)]
    other_z = 1 - z_hi
    remote(
        w_p_hbm.at[own_slice], w_p.at[other_z, x, own_slice], slice_base, pair_device
    ).wait()

    @pl.loop(1, 4)
    def _(d):
        slice_copy(other_z, d, x).start()

    for copy in loads[2:]:
        copy.start()

    query_scale = HEAD_DIM ** (-0.5) * math.log2(math.e)
    got_q.wait()

    def make_queries(first, last):
        @pl.loop(first, last)
        def _(c):
            here = pl.ds(pl.multiple_of(c * 128, 128), 128)
            normed = norm_rows(tok[here].astype(F32)).astype(BF16)
            q_ref[here] = (dot(normed, w_q[...]) * query_scale).astype(BF16)

    make_queries(0, 4)

    @pl.loop(1, N_SEQ)
    def _(d):
        to = (seq + d) % N_SEQ
        source = (seq + N_SEQ - d) % N_SEQ
        remote(
            pick_out.at[pick_rows(to)], pick_in.at[pick_rows(source)], pick_base + d, at_seq(to)
        ).wait()

    slot = lax.broadcasted_iota(jnp.int32, (2 * block_rows, 256), 0)
    lane = lax.broadcasted_iota(jnp.int32, (2 * block_rows, 256), 1)
    wanted = (slot * 128 + seq * 8 + tp).astype(F32)
    live = (wanted >= lane_before) & (wanted < lane_before + lane_count)
    live = live & ((lane & 7) == (slot & 7))
    for h in range(2):
        chosen = (live & (((lane >> 3) & 1) == h)).astype(F32).astype(BF16)
        own_rows[:, h * half_width : (h + 1) * half_width] = dot(chosen, pick_in[...])

    def own_block(ref, a, ring, pair):
        first = tp_of(ring, pair) * block_rows
        return ref.at[a, pl.ds(pl.multiple_of(first, block_rows), block_rows)]

    def tp_device(ring, pair):
        return at_tp(tp_of(ring, pair))

    mine = pl.ds(pl.multiple_of(tp * block_rows, block_rows), block_rows)
    halves = [slice(a * block_rows, (a + 1) * block_rows) for a in range(2)]
    gather_in = []
    for a in range(2):
        enc_in[a, mine] = norm_rows(own_rows[halves[a]]).astype(BF16)
        gather_in.append(
            RingGather(sems, x, z_hi, functools.partial(own_block, enc_in, a), tp_device)
        )
        gather_in[a].start()

    def w_block(ring, which, half=None):
        if half is None:
            return w_p.at[:, :, slice_of(ring, which)]
        return w_p.at[half, :, slice_of(ring, which)]

    def seq_device(ring, pair):
        return at_seq(seq_of(ring, pair, core))

    other_core = at_seq(seq_of(y, z_lo, 1 - core))
    up, down = seq_device(y + 1, z_lo), seq_device(y + 3, z_lo)
    w_base = sems.take(8)

    def w_copy(i, ring, which=None, half=None):
        ref = w_block(ring, core if which is None else which, half)
        return remote(ref, ref, w_base + i, (up, down, up, down)[i] if i < 4 else other_core)

    def w_start():
        got_p.wait()

        @pl.loop(1, 4)
        def _(d):
            slice_copy(z_hi, d, (x + 4 - d) % 4).wait()

        @pl.loop(1, 4)
        def _(d):
            slice_copy(other_z, d, (x + 4 - d) % 4).wait()

        w_copy(0, y).start()
        w_copy(1, y).start()
        w_copy(4, y).start()

    def w_sides():
        w_copy(0, y + 3).wait_recv()
        w_copy(2, y + 3, half=0).start()
        w_copy(5, y + 3).start()
        w_copy(1, y + 1).wait_recv()
        w_copy(3, y + 1, half=1).start()
        w_copy(6, y + 1).start()

    def w_far():
        w_copy(2, y + 2, half=0).wait_recv()
        w_copy(3, y + 2, half=1).wait_recv()
        w_copy(7, y + 2).start()
        for i, ring in enumerate((y, y + 3, y + 1, y + 2)):
            w_copy(4 + i, ring, 1 - core).wait_recv()

    def w_drain():
        for i, ring in enumerate((y, y, y + 3, y + 1, y, y + 3, y + 1, y + 2)):
            w_copy(i, ring, half=(None, None, 0, 1)[i] if i < 4 else None).wait_send()

    def to_hidden(a):
        @pl.loop(0, hidden.shape[2] // 256)
        def _(c):
            here = pl.ds(pl.multiple_of(c * 256, 256), 256)
            hidden[a, :, here] = jax.nn.gelu(dot(enc_in[a], w_in[:, here])).astype(BF16)

    def to_part(a):
        @pl.loop(0, width // 256)
        def _(c):
            here = pl.ds(pl.multiple_of(c * 256, 256), 256)
            part_out[a, :, here] = dot(hidden[a], w_out[:, here]).astype(BF16)

    slab_rows = 2 * block_rows
    low, high = pl.ds(0, half_width), pl.ds(half_width, half_width)
    sum_base = [sems.take(7), sems.take(7)]
    right, left = at_tp(tp_of(x + 1, z_hi)), at_tp(tp_of(x + 3, z_hi))

    def slab(ring):
        return pl.ds(pl.multiple_of((ring % 4) * slab_rows, slab_rows), slab_rows)

    def of_pair(pair):
        return pl.ds(pl.multiple_of(pair * block_rows, block_rows), block_rows)

    def of_both(pair):
        first = (x * 2 + pair) * block_rows
        return pl.ds(pl.multiple_of(first, block_rows), block_rows)

    def sum_copy(a, i):
        part, side = part_out.at[a], side_in.at[a]
        src, dst, to = (
            lambda: (part.at[slab(x + 2), low], far_in.at[a, 0], right),
            lambda: (part.at[slab(x + 2), high], far_in.at[a, 1], left),
            lambda: (part.at[slab(x + 1), high], side.at[0, :, high], right),
            lambda: (part.at[slab(x + 3), low], side.at[1, :, low], left),
            lambda: (both_out.at[a, 0], side.at[0, :, low], right),
            lambda: (both_out.at[a, 1], side.at[1, :, high], left),
            lambda: (pair_out.at[a], pair_in.at[a], at_tp(tp_of(x, 1 - z_hi))),
        )[i]()
        return remote(src, dst, sum_base[a] + i, to)

    def sum_start(a):
        for i in range(2):
            sum_copy(a, i).start()

    def sum_sides(a):
        for i in range(2, 4):
            sum_copy(a, i).start()

    def sum_add(a):
        for i, (ring, columns) in enumerate(((x + 1, low), (x + 3, high))):
            sum_copy(a, i).wait_recv()
            own = part_out[a, slab(ring), columns].astype(F32)
            both_out[a, i] = (own + far_in[a, i].astype(F32)).astype(BF16)
            sum_copy(a, 4 + i).start()

    def sum_of_pair(a, pair):
        total = part_out[a, of_both(pair)].astype(F32)
        return total + sum(side_in[a, i, of_pair(pair)].astype(F32) for i in range(2))

    def sum_swap(a):
        for i in range(2, 6):
            sum_copy(a, i).wait_recv()
        pair_out[a] = sum_of_pair(a, 1 - z_hi).astype(BF16)
        sum_copy(a, 6).start()

    gather_key = [
        RingGather(sems, x, z_hi, functools.partial(own_block, key_in, a), tp_device)
        for a in range(2)
    ]

    def sum_end(a):
        total = own_rows[halves[a]] + sum_of_pair(a, z_hi)
        sum_copy(a, 6).wait_recv()
        encoded = (total + pair_in[a].astype(F32)).astype(BF16).astype(F32)
        key_in[a, mine] = norm_rows(encoded).astype(BF16)
        gather_key[a].start()

    kv_width = w_k.shape[1]
    own = seq_of(y, z_lo, core)

    def kv_block(a, ring, pair, which):
        return kv.at[seq_of(ring, pair, which), a]

    def half_of(ref, half):
        return ref.at[pl.ds(half * (group // 2), group // 2)]

    def kv_gather(a):
        return RingGather(
            sems,
            y,
            z_lo,
            lambda ring, pair: kv_block(a, ring, pair, core),
            seq_device,
            half=half_of if a == 0 else None,
        )

    gather_kv = [kv_gather(a) for a in range(2)]
    share_kv = [
        CoreShare(sems, functools.partial(kv_block, a), core, other_core) for a in range(2)
    ]

    def to_kv(a):
        kv[own, a, :, :kv_width] = dot(key_in[a], w_k[...]).astype(BF16)
        kv[own, a, :, kv_width:] = dot(key_in[a], w_v[...]).astype(BF16)
        gather_kv[a].start()
        share_kv[a].send(0, y, z_lo)

    def kv_partner(a):
        gather_kv[a].partner()
        share_kv[a].send(1, y, 1 - z_lo)

    def kv_sides(a):
        gather_kv[a].sides()
        share_kv[a].send(2, y + 3, z_lo)
        share_kv[a].send(3, y + 1, z_lo)

    def kv_partner_sides(a):
        gather_kv[a].partner_sides()
        share_kv[a].send(4, y + 3, 1 - z_lo)
        share_kv[a].send(5, y + 1, 1 - z_lo)

    def kv_far(a):
        gather_kv[a].far()
        share_kv[a].send(6, y + 2, z_lo)

    def kv_partner_far(a):
        gather_kv[a].partner_far()
        share_kv[a].send(7, y + 2, 1 - z_lo)

    ones = jnp.ones((group, HEAD_DIM), BF16)

    def attend(here, a, blocks):
        for h in range(2):
            cols = slice(h * HEAD_DIM, (h + 1) * HEAD_DIM)
            v_cols = slice(kv_width + h * HEAD_DIM, kv_width + (h + 1) * HEAD_DIM)
            keys = jnp.concatenate([kv[b, a, :, cols] for b in blocks], axis=0)
            values = jnp.concatenate(
                [jnp.concatenate([kv[b, a, :, v_cols], ones], axis=1) for b in blocks], axis=0
            )
            scores = dot_t(q_ref[here, cols], keys)
            old = top_ref[h, here]
            new = jnp.maximum(old, jnp.max(scores, axis=1, keepdims=True))
            shrink = jnp.exp2(old - new)
            spread = jnp.concatenate([new] * (scores.shape[1] // HEAD_DIM), axis=1)
            weights = jnp.exp2(scores - spread)
            top_ref[h, here] = new
            acc_ref[h, here] = acc_ref[h, here] * jnp.concatenate([shrink] * 2, axis=1) + dot(
                weights.astype(BF16), values
            )

    pairs = (
        ((y, z_lo), (y, 1 - z_lo)),
        ((y + 3, z_lo), (y + 1, z_lo)),
        ((y + 3, 1 - z_lo), (y + 1, 1 - z_lo)),
        ((y + 2, z_lo), (y + 2, 1 - z_lo)),
    )

    def blocks_of(step):
        places = pairs[2 * step] + pairs[2 * step + 1]
        return [seq_of(*place, c) for place in places for c in (core, 1 - core)]

    def share_wait(a, step):
        for i in range(4):
            share_kv[a].wait(4 * step + i, *pairs[2 * step + i // 2][i % 2])

    def attend_all(a, step):
        share_wait(a, step)
        blocks = blocks_of(step)

        @pl.loop(0, rows // 512)
        def _(c):
            attend(pl.ds(pl.multiple_of(c * 512, 512), 512), a, blocks)


    def transpose_own():
        part = width // N_TP
        both_cols = pl.ds(pl.multiple_of(x * 2 * part, 2 * part), 2 * part)

        @pl.loop(0, rows // 128)
        def _(c):
            here = pl.ds(pl.multiple_of(c * 128, 128), 128)
            wide = tok[here, both_cols].astype(F32)
            own_cols[:, here] = jnp.where(z_hi == 0, wide[:, :part], wide[:, part:]).T.astype(BF16)

    make_queries(4, 6)
    w_start()
    gather_in[0].partner()
    gather_in[0].sides()
    gather_in[0].far()
    gather_in[1].partner()
    gather_in[1].sides()
    gather_in[1].far()
    gather_in[0].partner_sides()
    got_in.wait()
    gather_in[0].partner_far()
    to_hidden(0)
    got_out.wait()
    to_part(0)
    sum_start(0)
    gather_in[1].partner_sides()
    gather_in[1].partner_far()
    to_hidden(1)
    sum_sides(0)
    to_part(1)
    sum_add(0)
    sum_start(1)
    sum_swap(0)
    sum_sides(1)
    sum_add(1)
    sum_end(0)
    sum_swap(1)
    make_queries(6, 8)
    transpose_own()
    gather_key[0].partner()
    gather_key[0].sides()
    gather_key[0].far()
    sum_end(1)
    gather_key[0].partner_sides()
    got_k.wait()
    got_v.wait()
    gather_key[0].partner_far()
    to_kv(0)
    gather_key[1].partner()
    gather_key[1].sides()
    gather_key[1].far()
    kv_sides(0)
    kv_partner(0)
    kv_far(0)
    gather_key[1].partner_sides()
    gather_key[1].partner_far()
    to_kv(1)
    top_ref[...] = jnp.full(top_ref.shape, -1e30, F32)
    acc_ref[...] = jnp.zeros(acc_ref.shape, F32)
    kv_partner_sides(0)
    kv_partner_far(0)
    attend_all(0, 0)
    kv_partner(1)
    kv_sides(1)
    kv_far(1)
    w_sides()
    attend_all(0, 1)
    kv_partner_sides(1)
    kv_partner_far(1)
    attend_all(1, 0)
    share_wait(1, 1)

    att_base = sems.take(8)
    last_blocks = blocks_of(1)

    def att_copy(i, b, to, source, of):
        return pltpu.make_async_remote_copy(
            src_ref=att_out.at[to],
            dst_ref=att_in.at[source],
            send_sem=send_sem.at[att_base + i * 2 + b],
            recv_sem=recv_sem.at[att_base + i * 2 + of],
            device_id=at_tp(to),
            device_id_type=MESH,
        )

    @pl.loop(0, 4)
    def _(i):
        ring = (x + 1 + i) % 4
        here = pl.ds(pl.multiple_of(ring * 256, 256), 256)
        attend(here, 1, last_blocks)
        for h in range(2):
            done = acc_ref[h, here]
            done = (done[:, :HEAD_DIM] / done[:, HEAD_DIM:]).astype(BF16)
            cols = slice(h * HEAD_DIM, (h + 1) * HEAD_DIM)
            att_out[pl.ds(tp_of(ring, 0), 2), :, cols] = done.reshape(2, 128, HEAD_DIM)

        @pl.when(i < 3)
        def _():
            for b in range(2):
                att_copy(i, b, tp_of(ring, b), tp, z_hi).start()

    to_pair = tp_of(x, 1 - z_hi)
    att_copy(3, 0, to_pair, tp, 0).start()
    att_in[pl.ds(tp, 1)] = att_out[pl.ds(tp, 1)]

    w_far()

    @pl.loop(0, 3)
    def _(i):
        for b in range(2):
            to = tp_of(x + 1 + i, b)
            source = tp_of(x + 3 - i, b)
            copy = att_copy(i, b, to, source, b)
            copy.wait_send()
            copy.wait_recv()

    att_copy(3, 0, to_pair, to_pair, 0).wait()

    part = width // N_TP
    res_base = sems.take(8)
    stat_base = sems.take(N_TP)

    def res_copy(i, b, to, source, of):
        return pltpu.make_async_remote_copy(
            src_ref=res_out.at[to],
            dst_ref=res_in.at[source],
            send_sem=send_sem.at[res_base + i * 2 + b],
            recv_sem=recv_sem.at[res_base + i * 2 + of],
            device_id=at_tp(to),
            device_id_type=MESH,
        )

    @pl.loop(0, 4)
    def _(i):
        ring = (x + 1 + i) % 4
        here = pl.ds(pl.multiple_of(ring * 2 * part, 2 * part), 2 * part)
        total = dot(att_in[0], w_p[0, 0, :, here])
        for t in range(1, N_TP):
            total = total + dot(att_in[t], w_p[t % 2, t // 2, :, here])
        proj[:, here] = total
        for b in range(2):
            block = total[:, b * part : (b + 1) * part].T.astype(BF16)
            res_out[pl.ds(tp_of(ring, b), 1)] = block[None]

        @pl.when(i < 3)
        def _():
            for b in range(2):
                res_copy(i, b, tp_of(ring, b), tp, z_hi).start()

    res_copy(3, 0, to_pair, tp, 0).start()
    res_in[pl.ds(tp, 1)] = res_out[pl.ds(tp, 1)]
    row_mean = jnp.mean(proj[...], axis=1, keepdims=True)
    centred = proj[...] - row_mean
    scale = lax.rsqrt(jnp.mean(centred * centred, axis=1, keepdims=True) + EPSILON)
    lane = lax.broadcasted_iota(jnp.int32, (HEAD_DIM, HEAD_DIM), 1)
    stat_out[...] = jnp.where(lane == 0, row_mean, scale).T[:8]

    def stat_copy(d, source):
        return remote(stat_out, stat_in.at[source], stat_base + d, at_tp((tp + d) % N_TP))

    @pl.loop(1, N_TP)
    def _(d):
        stat_copy(d, tp).start()

    stat_in[pl.ds(tp, 1)] = stat_out[...][None]

    def finish(source):
        here = pl.ds(pl.multiple_of(source * HEAD_DIM, HEAD_DIM), HEAD_DIM)
        stats = stat_in[source]
        normal = (res_in[source].astype(F32) - stats[:1]) * stats[1:2]
        result[:, here] = own_cols[:, here].astype(F32) + normal
        copy = pltpu.make_async_copy(
            result.at[:, here], out_ref.at[:, here], local_sem.at[8 + source]
        )
        copy.start()

    finish(tp)

    @pl.loop(1, N_TP)
    def _(d):
        stat_copy(d, (tp + N_TP - d) % N_TP).wait()

    res_copy(3, 0, to_pair, to_pair, 0).wait()
    finish(to_pair)

    @pl.loop(0, 3)
    def _(i):
        for b in range(2):
            source = tp_of(x + 3 - i, b)
            copy = res_copy(i, b, tp_of(x + 1 + i, b), source, b)
            copy.wait_send()
            copy.wait_recv()
            finish(source)

    @pl.loop(0, N_TP)
    def _(t):
        here = pl.ds(pl.multiple_of(t * HEAD_DIM, HEAD_DIM), HEAD_DIM)
        pltpu.make_async_copy(
            result.at[:, here], out_ref.at[:, here], local_sem.at[8 + t]
        ).wait()

    for transfer in (*gather_in, *gather_key, *gather_kv, *share_kv):
        transfer.drain()
    for a in range(2):
        for i in range(7):
            sum_copy(a, i).wait_send()
    w_drain()


def shards(tokens, visible, w_in, w_out, w_query, w_key, w_value, w_proj):
    rows, width = tokens.shape
    part = width // N_TP
    block_rows = rows // 64
    group = block_rows * N_TP
    any_spec = pl.BlockSpec(memory_space=pl.ANY)
    vmem_spec = pl.BlockSpec(memory_space=pltpu.VMEM)
    heads = w_query.shape[1]
    result = pl.pallas_call(
        kernel,
        out_shape=jax.ShapeDtypeStruct((part, rows), F32),
        in_specs=[vmem_spec] * 2 + [any_spec] * 7,
        out_specs=any_spec,
        scratch_shapes=[
            pltpu.VMEM(tokens.shape, BF16),
            pltpu.VMEM(w_in.shape, BF16),
            pltpu.VMEM(w_out.shape, BF16),
            pltpu.VMEM(w_query.shape, BF16),
            pltpu.VMEM(w_key.shape, BF16),
            pltpu.VMEM(w_value.shape, BF16),
            pltpu.VMEM((2, 4, *w_proj.shape), BF16),
            pltpu.VMEM((N_SEQ, 8, rows // 8), jnp.int32),
            pltpu.VMEM((16 * N_SEQ, width // 2), BF16),
            pltpu.VMEM((16 * N_SEQ, width // 2), BF16),
            pltpu.VMEM((2 * block_rows, width), F32),
            pltpu.VMEM((2, group, width), BF16),
            pltpu.VMEM((2, group, w_in.shape[1]), BF16),
            pltpu.VMEM((2, group, width), BF16),
            pltpu.VMEM((2, 2, 2 * block_rows, width // 2), BF16),
            pltpu.VMEM((2, 2, 2 * block_rows, width // 2), BF16),
            pltpu.VMEM((2, 2, 2 * block_rows, width), BF16),
            pltpu.VMEM((2, block_rows, width), BF16),
            pltpu.VMEM((2, block_rows, width), BF16),
            pltpu.VMEM((2, group, width), BF16),
            pltpu.VMEM((N_SEQ, 2, group, 2 * heads), BF16),
            pltpu.VMEM((rows, heads), BF16),
            pltpu.VMEM((2, rows, HEAD_DIM), F32),
            pltpu.VMEM((2, rows, 2 * HEAD_DIM), F32),
            pltpu.VMEM((N_TP, rows // N_TP, heads), BF16),
            pltpu.VMEM((N_TP, rows // N_TP, heads), BF16),
            pltpu.VMEM((rows // N_TP, width), F32),
            pltpu.VMEM((N_TP, part, rows // N_TP), BF16),
            pltpu.VMEM((N_TP, part, rows // N_TP), BF16),
            pltpu.VMEM((8, rows // N_TP), F32),
            pltpu.VMEM((N_TP, 8, rows // N_TP), F32),
            pltpu.VMEM((part, rows), BF16),
            pltpu.VMEM((part, rows), F32),
            pltpu.SemaphoreType.DMA((16,)),
            pltpu.SemaphoreType.DMA((160,)),
            pltpu.SemaphoreType.DMA((160,)),
        ],
        compiler_params=pltpu.CompilerParams(
            collective_id=0, has_side_effects=True, vmem_limit_bytes=60 * 1024 * 1024
        ),
        name="generator_step",
    )(
        visible.reshape(8, rows // 8),
        visible.reshape(1, rows),
        tokens,
        w_in,
        w_out,
        w_query,
        w_key,
        w_value,
        w_proj,
    )
    return result.T


def solution(mesh):
    in_specs = (
        P("seq", None),
        P("seq"),
        P(None, "tp"),
        P("tp", None),
        P(None, "tp"),
        P(None, "tp"),
        P(None, "tp"),
        P("tp", None),
    )
    out_specs = P("seq", "tp")
    return jax.shard_map(shards, mesh=mesh, in_specs=in_specs, out_specs=out_specs, check_vma=False)
```

```python
import functools
import math

import jax
import jax.numpy as jnp
from jax import lax
from jax.experimental import pallas as pl
from jax.experimental.pallas import tpu as pltpu
from jax.sharding import PartitionSpec as P

HEAD_DIM = 128
EPSILON = 1e-05
MESH = pl.DeviceIdType.MESH
F32 = jnp.float32
BF16 = jnp.bfloat16
N_SEQ = 16
N_TP = 8


def norm_rows(values):
    row_mean = jnp.mean(values, axis=-1, keepdims=True)
    centred = values - row_mean
    variance = jnp.mean(centred * centred, axis=-1, keepdims=True)
    return centred * lax.rsqrt(variance + EPSILON)


def dot(a, b):
    return jnp.dot(a, b, preferred_element_type=F32)


def dot_t(a, b):
    return lax.dot_general(a, b, (((1,), (1,)), ((), ())), preferred_element_type=F32)


class Sems:
    def __init__(self, send, recv):
        self.send, self.recv, self.used = send, recv, 0

    def take(self, count):
        first = self.used
        self.used += count
        return first


class RingGather:
    def __init__(self, sems, ring, pair, block, device, half=None):
        self.sems, self.ring, self.pair, self.half = sems, ring, pair, half
        self.block, self.device = block, device
        self.base = sems.take(8)
        self.sent = []

    def _copy(self, i, ring, pair, device):
        ref = self.block(ring, pair)
        if self.half is not None and i in (3, 7):
            ref = self.half(ref, i // 7)
        return pltpu.make_async_remote_copy(
            src_ref=ref,
            dst_ref=ref,
            send_sem=self.sems.send.at[self.base + i],
            recv_sem=self.sems.recv.at[self.base + i],
            device_id=device,
            device_id_type=MESH,
        )

    def _send(self, i, ring, pair, to_ring, to_pair):
        copy = self._copy(i, ring, pair, self.device(to_ring, to_pair))
        copy.start()
        self.sent.append(copy)

    def _wait(self, i, ring, pair):
        self._copy(i, ring, pair, self.device(self.ring, 1 - self.pair)).wait_recv()

    def start(self):
        r, p = self.ring, self.pair
        self._send(0, r, p, r, 1 - p)
        self._send(1, r, p, r + 1, p)
        self._send(2, r, p, r + 3, p)
        if self.half is None:
            self._send(3, r, p, r + 2, p)

    def partner(self):
        r, p = self.ring, self.pair
        self._wait(0, r, 1 - p)
        self._send(4, r, 1 - p, r + 1, p)
        self._send(5, r, 1 - p, r + 3, p)

    def sides(self):
        r, p = self.ring, self.pair
        self._wait(1, r + 3, p)
        if self.half is not None:
            self._send(3, r + 3, p, r + 1, p)
        self._wait(2, r + 1, p)
        if self.half is not None:
            self._send(7, r + 1, p, r + 3, p)

    def far(self):
        r, p = self.ring, self.pair
        self._wait(3, r + 2, p)
        if self.half is not None:
            self._wait(7, r + 2, p)
        self._send(6, r + 2, p, r, 1 - p)

    def partner_sides(self):
        self._wait(4, self.ring + 3, 1 - self.pair)
        self._wait(5, self.ring + 1, 1 - self.pair)

    def partner_far(self):
        self._wait(6, self.ring + 2, 1 - self.pair)

    def drain(self):
        for copy in self.sent:
            copy.wait_send()


class CoreShare:
    def __init__(self, sems, block, core, device):
        self.sems, self.block, self.core, self.device = sems, block, core, device
        self.base = sems.take(8)
        self.sent = []

    def _copy(self, i, ring, pair, core):
        ref = self.block(ring, pair, core)
        return pltpu.make_async_remote_copy(
            src_ref=ref,
            dst_ref=ref,
            send_sem=self.sems.send.at[self.base + i],
            recv_sem=self.sems.recv.at[self.base + i],
            device_id=self.device,
            device_id_type=MESH,
        )

    def send(self, i, ring, pair):
        copy = self._copy(i, ring, pair, self.core)
        copy.start()
        self.sent.append(copy)

    def wait(self, i, ring, pair):
        self._copy(i, ring, pair, 1 - self.core).wait_recv()

    def drain(self):
        for copy in self.sent:
            copy.wait_send()


def kernel(
    vis_tile,
    vis_row,
    tok_hbm,
    w_in_hbm,
    w_out_hbm,
    w_q_hbm,
    w_k_hbm,
    w_v_hbm,
    w_p_hbm,
    out_ref,
    tok,
    w_in,
    w_out,
    w_q,
    w_k,
    w_v,
    w_p,
    counts,
    pick_out,
    pick_in,
    own_rows,
    enc_in,
    hidden,
    part_out,
    far_in,
    both_out,
    side_in,
    pair_out,
    pair_in,
    key_in,
    kv,
    q_ref,
    top_ref,
    acc_ref,
    att_out,
    att_in,
    proj,
    res_out,
    res_in,
    stat_out,
    stat_in,
    own_cols,
    result,
    local_sem,
    send_sem,
    recv_sem,
):
    rows, width = tok.shape
    seq = lax.axis_index("seq")
    tp = lax.axis_index("tp")
    core, z_lo, y = seq % 2, (seq // 2) % 2, seq // 4
    x, z_hi = tp // 2, tp % 2
    sems = Sems(send_sem, recv_sem)
    block_rows = own_rows.shape[0] // 2
    group = block_rows * N_TP
    half_width = width // 2

    def at_seq(index):
        return {"seq": index, "tp": tp}

    def at_tp(index):
        return {"seq": seq, "tp": index}

    def seq_of(ring, pair, which):
        return ((ring % 4) * 2 + pair) * 2 + which

    def tp_of(ring, pair):
        return (ring % 4) * 2 + pair

    slice_rows = w_p.shape[2] // 8

    def slice_of(ring, which):
        return pl.ds(pl.multiple_of(((ring % 4) * 2 + which) * slice_rows, slice_rows), slice_rows)

    own_slice = slice_of(y, core)
    loads = [
        pltpu.make_async_copy(src, dst, local_sem.at[i])
        for i, (src, dst) in enumerate(
            (
                (tok_hbm, tok),
                (w_p_hbm.at[own_slice], w_p.at[z_hi, x, own_slice]),
                (w_q_hbm, w_q),
                (w_in_hbm, w_in),
                (w_out_hbm, w_out),
                (w_k_hbm, w_k),
                (w_v_hbm, w_v),
            )
        )
    ]
    got_tok, got_p, got_q, got_in, got_out, got_k, got_v = loads
    for copy in loads[:2]:
        copy.start()

    barrier = pltpu.get_barrier_semaphore()

    @pl.loop(1, N_SEQ)
    def _(d):
        pl.semaphore_signal(
            barrier, inc=1, device_id=at_seq((seq + d) % N_SEQ), device_id_type=MESH
        )

    @pl.loop(1, N_TP)
    def _(d):
        pl.semaphore_signal(barrier, inc=1, device_id=at_tp((tp + d) % N_TP), device_id_type=MESH)

    visible = vis_row[...].astype(F32)
    lower = (
        lax.broadcasted_iota(jnp.int32, (rows, rows), 0)
        <= lax.broadcasted_iota(jnp.int32, (rows, rows), 1)
    ).astype(F32).astype(BF16)
    upto = dot(jnp.broadcast_to(visible, (8, rows)).astype(BF16), lower)[:1]

    pl.semaphore_wait(barrier, N_SEQ + N_TP - 2)

    def remote(src, dst, index, device):
        return pltpu.make_async_remote_copy(
            src_ref=src,
            dst_ref=dst,
            send_sem=send_sem.at[index],
            recv_sem=recv_sem.at[index],
            device_id=device,
            device_id_type=MESH,
        )

    count_base = sems.take(N_SEQ)

    @pl.loop(1, N_SEQ)
    def _(d):
        remote(
            vis_tile, counts.at[seq], count_base + d, at_seq((seq + d) % N_SEQ)
        ).start()

    counts[pl.ds(seq, 1)] = vis_tile[...][None]

    slice_base = sems.take(8)
    pair_device = at_tp(tp_of(x, 1 - z_hi))
    remote(
        w_p_hbm.at[own_slice], w_p.at[z_hi, x, own_slice], slice_base, pair_device
    ).start()

    def slice_copy(of, d, ring):
        here = w_p.at[of, ring, own_slice]
        src = w_p_hbm.at[own_slice] if of is z_hi else w_p.at[of, x, own_slice]
        index = slice_base + d + (0 if of is z_hi else 4)
        return remote(src, here, index, at_tp(tp_of(x + d, z_hi)))

    @pl.loop(1, 4)
    def _(d):
        slice_copy(z_hi, d, x).start()

    @pl.loop(1, N_SEQ)
    def _(d):
        remote(
            vis_tile, counts.at[(seq + N_SEQ - d) % N_SEQ], count_base + d, at_seq((seq + d) % N_SEQ)
        ).wait()

    lane_source = lax.broadcasted_iota(jnp.int32, (1, 256), 1) // 16
    before_me = jnp.zeros((1, 1), F32)
    lane_before = jnp.zeros((1, 256), F32)
    lane_count = jnp.zeros((1, 256), F32)
    for s in range(N_SEQ):
        count = jnp.sum(counts[s].astype(F32), axis=1, keepdims=True)
        count = jnp.sum(count, axis=0, keepdims=True)
        before_me = before_me + jnp.where(seq > s, 1.0, 0.0) * count
        lane_before = lane_before + jnp.where(lane_source > s, count, 0.0)
        lane_count = lane_count + jnp.where(lane_source == s, count, 0.0)

    rank = (before_me + upto - 1.0).astype(jnp.int32)
    code = ((rank >> 3) & 15) * 8 + ((rank >> 7) & 7)
    code = jnp.where((visible > 0.0) & ((rank & 7) == tp), code, -1)
    picks = (lax.broadcasted_iota(jnp.int32, (128, rows), 0) == code).astype(F32).astype(BF16)
    got_tok.wait()
    for h in range(2):
        for c in range(0, half_width, 640):
            rows_of = dot(picks, tok[:, h * half_width + c : h * half_width + c + 640])
            rows_of = rows_of.reshape(16, 8, 640)
            if h == 0:
                proj[:, c : c + 640] = rows_of.reshape(128, 640)
            else:
                first = proj[:, c : c + 640].reshape(16, 8, 640)
                both = jnp.concatenate([first, rows_of], axis=1)
                pick_out[:, c : c + 640] = both.reshape(256, 640).astype(BF16)

    pick_base = sems.take(N_SEQ)

    def pick_rows(index):
        return pl.ds(pl.multiple_of(index * 16, 16), 16)

    @pl.loop(1, N_SEQ)
    def _(d):
        to = (seq + d) % N_SEQ
        remote(
            pick_out.at[pick_rows(to)], pick_in.at[pick_rows(seq)], pick_base + d, at_seq(to)
        ).start()

    pick_in[pick_rows(seq)] = pick_out[pick_rows(seq)]
    other_z = 1 - z_hi
    remote(
        w_p_hbm.at[own_slice], w_p.at[other_z, x, own_slice], slice_base, pair_device
    ).wait()

    @pl.loop(1, 4)
    def _(d):
        slice_copy(other_z, d, x).start()

    for copy in loads[2:]:
        copy.start()

    query_scale = HEAD_DIM ** (-0.5) * math.log2(math.e)
    got_q.wait()

    def make_queries(first, last):
        @pl.loop(first, last)
        def _(c):
            here = pl.ds(pl.multiple_of(c * 128, 128), 128)
            normed = norm_rows(tok[here].astype(F32)).astype(BF16)
            q_ref[here] = (dot(normed, w_q[...]) * query_scale).astype(BF16)

    make_queries(0, 4)

    @pl.loop(1, N_SEQ)
    def _(d):
        to = (seq + d) % N_SEQ
        source = (seq + N_SEQ - d) % N_SEQ
        remote(
            pick_out.at[pick_rows(to)], pick_in.at[pick_rows(source)], pick_base + d, at_seq(to)
        ).wait()

    slot = lax.broadcasted_iota(jnp.int32, (2 * block_rows, 256), 0)
    lane = lax.broadcasted_iota(jnp.int32, (2 * block_rows, 256), 1)
    wanted = (slot * 128 + seq * 8 + tp).astype(F32)
    live = (wanted >= lane_before) & (wanted < lane_before + lane_count)
    live = live & ((lane & 7) == (slot & 7))
    for h in range(2):
        chosen = (live & (((lane >> 3) & 1) == h)).astype(F32).astype(BF16)
        own_rows[:, h * half_width : (h + 1) * half_width] = dot(chosen, pick_in[...])

    def own_block(ref, a, ring, pair):
        first = tp_of(ring, pair) * block_rows
        return ref.at[a, pl.ds(pl.multiple_of(first, block_rows), block_rows)]

    def tp_device(ring, pair):
        return at_tp(tp_of(ring, pair))

    mine = pl.ds(pl.multiple_of(tp * block_rows, block_rows), block_rows)
    halves = [slice(a * block_rows, (a + 1) * block_rows) for a in range(2)]
    gather_in = []
    for a in range(2):
        enc_in[a, mine] = norm_rows(own_rows[halves[a]]).astype(BF16)
        gather_in.append(
            RingGather(sems, x, z_hi, functools.partial(own_block, enc_in, a), tp_device)
        )
        gather_in[a].start()

    def seq_device(ring, pair):
        return at_seq(seq_of(ring, pair, core))

    other_core = at_seq(seq_of(y, z_lo, 1 - core))
    up, down = seq_device(y + 1, z_lo), seq_device(y + 3, z_lo)
    w_base = sems.take(11)

    def w_copy(i, ring, which=None):
        ref = w_p.at[:, :, slice_of(ring, core if which is None else which)]
        return remote(ref, ref, w_base + i, (up, down)[i] if i < 2 else other_core)

    def w_part(i, ring):
        ref = w_p.at[i, x, slice_of(ring, core)]
        return remote(ref, ref, w_base + 2 + i, (up, down)[i])

    def w_cross(d, block):
        ref = w_p.at[:, block, slice_of(y + 2, core)]
        return remote(ref, ref, w_base + 7 + d, at_tp(tp_of(x + d, z_hi)))

    def w_start():
        got_p.wait()

        @pl.loop(1, 4)
        def _(d):
            slice_copy(z_hi, d, (x + 4 - d) % 4).wait()

        @pl.loop(1, 4)
        def _(d):
            slice_copy(other_z, d, (x + 4 - d) % 4).wait()

        w_copy(0, y).start()
        w_copy(1, y).start()
        w_copy(4, y).start()

    def w_sides():
        w_copy(0, y + 3).wait_recv()
        w_part(0, y + 3).start()
        w_copy(5, y + 3).start()
        w_copy(1, y + 1).wait_recv()
        w_part(1, y + 1).start()
        w_copy(6, y + 1).start()

    def w_spread():
        w_part(0, y + 2).wait_recv()
        w_part(1, y + 2).wait_recv()

        @pl.loop(1, 4)
        def _(d):
            w_cross(d, x).start()

    def w_far():
        @pl.loop(1, 4)
        def _(d):
            w_cross(d, (x + 4 - d) % 4).wait_recv()

        w_copy(7, y + 2).start()
        for i, ring in enumerate((y, y + 3, y + 1, y + 2)):
            w_copy(4 + i, ring, 1 - core).wait_recv()

    def w_drain():
        for i, ring in ((0, y), (1, y), (4, y), (5, y + 3), (6, y + 1), (7, y + 2)):
            w_copy(i, ring).wait_send()
        w_part(0, y + 3).wait_send()
        w_part(1, y + 1).wait_send()

        @pl.loop(1, 4)
        def _(d):
            w_cross(d, x).wait_send()

    def to_hidden(a):
        @pl.loop(0, hidden.shape[2] // 256)
        def _(c):
            here = pl.ds(pl.multiple_of(c * 256, 256), 256)
            hidden[a, :, here] = jax.nn.gelu(dot(enc_in[a], w_in[:, here])).astype(BF16)

    def to_part(a):
        @pl.loop(0, width // 256)
        def _(c):
            here = pl.ds(pl.multiple_of(c * 256, 256), 256)
            part_out[a, :, here] = dot(hidden[a], w_out[:, here]).astype(BF16)

    slab_rows = 2 * block_rows
    low, high = pl.ds(0, half_width), pl.ds(half_width, half_width)
    sum_base = [sems.take(7), sems.take(7)]
    right, left = at_tp(tp_of(x + 1, z_hi)), at_tp(tp_of(x + 3, z_hi))

    def slab(ring):
        return pl.ds(pl.multiple_of((ring % 4) * slab_rows, slab_rows), slab_rows)

    def of_pair(pair):
        return pl.ds(pl.multiple_of(pair * block_rows, block_rows), block_rows)

    def of_both(pair):
        first = (x * 2 + pair) * block_rows
        return pl.ds(pl.multiple_of(first, block_rows), block_rows)

    def sum_copy(a, i):
        part, side = part_out.at[a], side_in.at[a]
        src, dst, to = (
            lambda: (part.at[slab(x + 2), low], far_in.at[a, 0], right),
            lambda: (part.at[slab(x + 2), high], far_in.at[a, 1], left),
            lambda: (part.at[slab(x + 1), high], side.at[0, :, high], right),
            lambda: (part.at[slab(x + 3), low], side.at[1, :, low], left),
            lambda: (both_out.at[a, 0], side.at[0, :, low], right),
            lambda: (both_out.at[a, 1], side.at[1, :, high], left),
            lambda: (pair_out.at[a], pair_in.at[a], at_tp(tp_of(x, 1 - z_hi))),
        )[i]()
        return remote(src, dst, sum_base[a] + i, to)

    def sum_start(a):
        for i in range(2):
            sum_copy(a, i).start()

    def sum_sides(a):
        for i in range(2, 4):
            sum_copy(a, i).start()

    def sum_add(a):
        for i, (ring, columns) in enumerate(((x + 1, low), (x + 3, high))):
            sum_copy(a, i).wait_recv()
            own = part_out[a, slab(ring), columns].astype(F32)
            both_out[a, i] = (own + far_in[a, i].astype(F32)).astype(BF16)
            sum_copy(a, 4 + i).start()

    def sum_of_pair(a, pair):
        total = part_out[a, of_both(pair)].astype(F32)
        return total + sum(side_in[a, i, of_pair(pair)].astype(F32) for i in range(2))

    def sum_swap(a):
        for i in range(2, 6):
            sum_copy(a, i).wait_recv()
        pair_out[a] = sum_of_pair(a, 1 - z_hi).astype(BF16)
        sum_copy(a, 6).start()

    gather_key = [
        RingGather(sems, x, z_hi, functools.partial(own_block, key_in, a), tp_device)
        for a in range(2)
    ]

    def sum_end(a):
        total = own_rows[halves[a]] + sum_of_pair(a, z_hi)
        sum_copy(a, 6).wait_recv()
        encoded = (total + pair_in[a].astype(F32)).astype(BF16).astype(F32)
        key_in[a, mine] = norm_rows(encoded).astype(BF16)
        gather_key[a].start()

    kv_width = w_k.shape[1]
    own = seq_of(y, z_lo, core)

    def kv_block(a, ring, pair, which):
        return kv.at[seq_of(ring, pair, which), a]

    def half_of(ref, half):
        return ref.at[pl.ds(half * (group // 2), group // 2)]

    def kv_gather(a):
        return RingGather(
            sems,
            y,
            z_lo,
            lambda ring, pair: kv_block(a, ring, pair, core),
            seq_device,
            half=half_of if a == 0 else None,
        )

    gather_kv = [kv_gather(a) for a in range(2)]
    share_kv = [
        CoreShare(sems, functools.partial(kv_block, a), core, other_core) for a in range(2)
    ]

    def to_kv(a):
        kv[own, a, :, :kv_width] = dot(key_in[a], w_k[...]).astype(BF16)
        kv[own, a, :, kv_width:] = dot(key_in[a], w_v[...]).astype(BF16)
        gather_kv[a].start()
        share_kv[a].send(0, y, z_lo)

    def kv_partner(a):
        gather_kv[a].partner()
        share_kv[a].send(1, y, 1 - z_lo)

    def kv_sides(a):
        gather_kv[a].sides()
        share_kv[a].send(2, y + 3, z_lo)
        share_kv[a].send(3, y + 1, z_lo)

    def kv_partner_sides(a):
        gather_kv[a].partner_sides()
        share_kv[a].send(4, y + 3, 1 - z_lo)
        share_kv[a].send(5, y + 1, 1 - z_lo)

    def kv_far(a):
        gather_kv[a].far()
        share_kv[a].send(6, y + 2, z_lo)

    def kv_partner_far(a):
        gather_kv[a].partner_far()
        share_kv[a].send(7, y + 2, 1 - z_lo)

    ones = jnp.ones((group, HEAD_DIM), BF16)

    def attend(here, a, blocks):
        for h in range(2):
            cols = slice(h * HEAD_DIM, (h + 1) * HEAD_DIM)
            v_cols = slice(kv_width + h * HEAD_DIM, kv_width + (h + 1) * HEAD_DIM)
            keys = jnp.concatenate([kv[b, a, :, cols] for b in blocks], axis=0)
            values = jnp.concatenate(
                [jnp.concatenate([kv[b, a, :, v_cols], ones], axis=1) for b in blocks], axis=0
            )
            scores = dot_t(q_ref[here, cols], keys)
            old = top_ref[h, here]
            new = jnp.maximum(old, jnp.max(scores, axis=1, keepdims=True))
            shrink = jnp.exp2(old - new)
            spread = jnp.concatenate([new] * (scores.shape[1] // HEAD_DIM), axis=1)
            weights = jnp.exp2(scores - spread)
            top_ref[h, here] = new
            acc_ref[h, here] = acc_ref[h, here] * jnp.concatenate([shrink] * 2, axis=1) + dot(
                weights.astype(BF16), values
            )

    pairs = (
        ((y, z_lo), (y, 1 - z_lo)),
        ((y + 3, z_lo), (y + 1, z_lo)),
        ((y + 3, 1 - z_lo), (y + 1, 1 - z_lo)),
        ((y + 2, z_lo), (y + 2, 1 - z_lo)),
    )

    def blocks_of(step):
        places = pairs[2 * step] + pairs[2 * step + 1]
        return [seq_of(*place, c) for place in places for c in (core, 1 - core)]

    def share_wait(a, step):
        for i in range(4):
            share_kv[a].wait(4 * step + i, *pairs[2 * step + i // 2][i % 2])

    def attend_all(a, step):
        share_wait(a, step)
        blocks = blocks_of(step)

        @pl.loop(0, rows // 512)
        def _(c):
            attend(pl.ds(pl.multiple_of(c * 512, 512), 512), a, blocks)


    def transpose_own():
        part = width // N_TP
        both_cols = pl.ds(pl.multiple_of(x * 2 * part, 2 * part), 2 * part)

        @pl.loop(0, rows // 128)
        def _(c):
            here = pl.ds(pl.multiple_of(c * 128, 128), 128)
            wide = tok[here, both_cols].astype(F32)
            own_cols[:, here] = jnp.where(z_hi == 0, wide[:, :part], wide[:, part:]).T.astype(BF16)

    make_queries(4, 6)
    w_start()
    gather_in[0].partner()
    gather_in[0].sides()
    gather_in[0].far()
    gather_in[1].partner()
    gather_in[1].sides()
    gather_in[1].far()
    gather_in[0].partner_sides()
    got_in.wait()
    gather_in[0].partner_far()
    to_hidden(0)
    got_out.wait()
    to_part(0)
    sum_start(0)
    gather_in[1].partner_sides()
    gather_in[1].partner_far()
    to_hidden(1)
    sum_sides(0)
    to_part(1)
    sum_add(0)
    sum_start(1)
    sum_swap(0)
    sum_sides(1)
    sum_add(1)
    sum_end(0)
    sum_swap(1)
    make_queries(6, 8)
    transpose_own()
    gather_key[0].partner()
    gather_key[0].sides()
    gather_key[0].far()
    sum_end(1)
    w_sides()
    gather_key[0].partner_sides()
    got_k.wait()
    got_v.wait()
    gather_key[0].partner_far()
    to_kv(0)
    gather_key[1].partner()
    gather_key[1].sides()
    gather_key[1].far()
    kv_sides(0)
    kv_partner(0)
    kv_far(0)
    gather_key[1].partner_sides()
    gather_key[1].partner_far()
    to_kv(1)
    w_spread()
    top_ref[...] = jnp.full(top_ref.shape, -1e30, F32)
    acc_ref[...] = jnp.zeros(acc_ref.shape, F32)
    kv_partner_sides(0)
    kv_partner_far(0)
    attend_all(0, 0)
    kv_partner(1)
    kv_sides(1)
    kv_far(1)
    attend_all(0, 1)
    kv_partner_sides(1)
    kv_partner_far(1)
    attend_all(1, 0)
    share_wait(1, 1)

    att_base = sems.take(8)
    last_blocks = blocks_of(1)

    def att_copy(i, b, to, source, of):
        return pltpu.make_async_remote_copy(
            src_ref=att_out.at[to],
            dst_ref=att_in.at[source],
            send_sem=send_sem.at[att_base + i * 2 + b],
            recv_sem=recv_sem.at[att_base + i * 2 + of],
            device_id=at_tp(to),
            device_id_type=MESH,
        )

    @pl.loop(0, 4)
    def _(i):
        ring = (x + 1 + i) % 4
        here = pl.ds(pl.multiple_of(ring * 256, 256), 256)
        attend(here, 1, last_blocks)
        for h in range(2):
            done = acc_ref[h, here]
            done = (done[:, :HEAD_DIM] / done[:, HEAD_DIM:]).astype(BF16)
            cols = slice(h * HEAD_DIM, (h + 1) * HEAD_DIM)
            att_out[pl.ds(tp_of(ring, 0), 2), :, cols] = done.reshape(2, 128, HEAD_DIM)

        @pl.when(i < 3)
        def _():
            for b in range(2):
                att_copy(i, b, tp_of(ring, b), tp, z_hi).start()

    to_pair = tp_of(x, 1 - z_hi)
    att_copy(3, 0, to_pair, tp, 0).start()
    att_in[pl.ds(tp, 1)] = att_out[pl.ds(tp, 1)]

    w_far()

    @pl.loop(0, 3)
    def _(i):
        for b in range(2):
            to = tp_of(x + 1 + i, b)
            source = tp_of(x + 3 - i, b)
            copy = att_copy(i, b, to, source, b)
            copy.wait_send()
            copy.wait_recv()

    att_copy(3, 0, to_pair, to_pair, 0).wait()

    part = width // N_TP
    res_base = sems.take(8)
    stat_base = sems.take(N_TP)

    def res_copy(i, b, to, source, of):
        return pltpu.make_async_remote_copy(
            src_ref=res_out.at[to],
            dst_ref=res_in.at[source],
            send_sem=send_sem.at[res_base + i * 2 + b],
            recv_sem=recv_sem.at[res_base + i * 2 + of],
            device_id=at_tp(to),
            device_id_type=MESH,
        )

    @pl.loop(0, 4)
    def _(i):
        ring = (x + 1 + i) % 4
        here = pl.ds(pl.multiple_of(ring * 2 * part, 2 * part), 2 * part)
        total = dot(att_in[0], w_p[0, 0, :, here])
        for t in range(1, N_TP):
            total = total + dot(att_in[t], w_p[t % 2, t // 2, :, here])
        proj[:, here] = total
        for b in range(2):
            block = total[:, b * part : (b + 1) * part].T.astype(BF16)
            res_out[pl.ds(tp_of(ring, b), 1)] = block[None]

        @pl.when(i < 3)
        def _():
            for b in range(2):
                res_copy(i, b, tp_of(ring, b), tp, z_hi).start()

    res_copy(3, 0, to_pair, tp, 0).start()
    res_in[pl.ds(tp, 1)] = res_out[pl.ds(tp, 1)]
    row_mean = jnp.mean(proj[...], axis=1, keepdims=True)
    centred = proj[...] - row_mean
    scale = lax.rsqrt(jnp.mean(centred * centred, axis=1, keepdims=True) + EPSILON)
    lane = lax.broadcasted_iota(jnp.int32, (HEAD_DIM, HEAD_DIM), 1)
    stat_out[...] = jnp.where(lane == 0, row_mean, scale).T[:8]

    def stat_copy(d, source):
        return remote(stat_out, stat_in.at[source], stat_base + d, at_tp((tp + d) % N_TP))

    @pl.loop(1, N_TP)
    def _(d):
        stat_copy(d, tp).start()

    stat_in[pl.ds(tp, 1)] = stat_out[...][None]

    def finish(source):
        here = pl.ds(pl.multiple_of(source * HEAD_DIM, HEAD_DIM), HEAD_DIM)
        stats = stat_in[source]
        normal = (res_in[source].astype(F32) - stats[:1]) * stats[1:2]
        result[:, here] = own_cols[:, here].astype(F32) + normal
        copy = pltpu.make_async_copy(
            result.at[:, here], out_ref.at[:, here], local_sem.at[8 + source]
        )
        copy.start()

    finish(tp)

    @pl.loop(1, N_TP)
    def _(d):
        stat_copy(d, (tp + N_TP - d) % N_TP).wait()

    res_copy(3, 0, to_pair, to_pair, 0).wait()
    finish(to_pair)

    @pl.loop(0, 3)
    def _(i):
        for b in range(2):
            source = tp_of(x + 3 - i, b)
            copy = res_copy(i, b, tp_of(x + 1 + i, b), source, b)
            copy.wait_send()
            copy.wait_recv()
            finish(source)

    @pl.loop(0, N_TP)
    def _(t):
        here = pl.ds(pl.multiple_of(t * HEAD_DIM, HEAD_DIM), HEAD_DIM)
        pltpu.make_async_copy(
            result.at[:, here], out_ref.at[:, here], local_sem.at[8 + t]
        ).wait()

    for transfer in (*gather_in, *gather_key, *gather_kv, *share_kv):
        transfer.drain()
    for a in range(2):
        for i in range(7):
            sum_copy(a, i).wait_send()
    w_drain()


def shards(tokens, visible, w_in, w_out, w_query, w_key, w_value, w_proj):
    rows, width = tokens.shape
    part = width // N_TP
    block_rows = rows // 64
    group = block_rows * N_TP
    any_spec = pl.BlockSpec(memory_space=pl.ANY)
    vmem_spec = pl.BlockSpec(memory_space=pltpu.VMEM)
    heads = w_query.shape[1]
    result = pl.pallas_call(
        kernel,
        out_shape=jax.ShapeDtypeStruct((part, rows), F32),
        in_specs=[vmem_spec] * 2 + [any_spec] * 7,
        out_specs=any_spec,
        scratch_shapes=[
            pltpu.VMEM(tokens.shape, BF16),
            pltpu.VMEM(w_in.shape, BF16),
            pltpu.VMEM(w_out.shape, BF16),
            pltpu.VMEM(w_query.shape, BF16),
            pltpu.VMEM(w_key.shape, BF16),
            pltpu.VMEM(w_value.shape, BF16),
            pltpu.VMEM((2, 4, *w_proj.shape), BF16),
            pltpu.VMEM((N_SEQ, 8, rows // 8), jnp.int32),
            pltpu.VMEM((16 * N_SEQ, width // 2), BF16),
            pltpu.VMEM((16 * N_SEQ, width // 2), BF16),
            pltpu.VMEM((2 * block_rows, width), F32),
            pltpu.VMEM((2, group, width), BF16),
            pltpu.VMEM((2, group, w_in.shape[1]), BF16),
            pltpu.VMEM((2, group, width), BF16),
            pltpu.VMEM((2, 2, 2 * block_rows, width // 2), BF16),
            pltpu.VMEM((2, 2, 2 * block_rows, width // 2), BF16),
            pltpu.VMEM((2, 2, 2 * block_rows, width), BF16),
            pltpu.VMEM((2, block_rows, width), BF16),
            pltpu.VMEM((2, block_rows, width), BF16),
            pltpu.VMEM((2, group, width), BF16),
            pltpu.VMEM((N_SEQ, 2, group, 2 * heads), BF16),
            pltpu.VMEM((rows, heads), BF16),
            pltpu.VMEM((2, rows, HEAD_DIM), F32),
            pltpu.VMEM((2, rows, 2 * HEAD_DIM), F32),
            pltpu.VMEM((N_TP, rows // N_TP, heads), BF16),
            pltpu.VMEM((N_TP, rows // N_TP, heads), BF16),
            pltpu.VMEM((rows // N_TP, width), F32),
            pltpu.VMEM((N_TP, part, rows // N_TP), BF16),
            pltpu.VMEM((N_TP, part, rows // N_TP), BF16),
            pltpu.VMEM((8, rows // N_TP), F32),
            pltpu.VMEM((N_TP, 8, rows // N_TP), F32),
            pltpu.VMEM((part, rows), BF16),
            pltpu.VMEM((part, rows), F32),
            pltpu.SemaphoreType.DMA((16,)),
            pltpu.SemaphoreType.DMA((160,)),
            pltpu.SemaphoreType.DMA((160,)),
        ],
        compiler_params=pltpu.CompilerParams(
            collective_id=0, has_side_effects=True, vmem_limit_bytes=60 * 1024 * 1024
        ),
        name="generator_step",
    )(
        visible.reshape(8, rows // 8),
        visible.reshape(1, rows),
        tokens,
        w_in,
        w_out,
        w_query,
        w_key,
        w_value,
        w_proj,
    )
    return result.T


def solution(mesh):
    in_specs = (
        P("seq", None),
        P("seq"),
        P(None, "tp"),
        P("tp", None),
        P(None, "tp"),
        P(None, "tp"),
        P(None, "tp"),
        P("tp", None),
    )
    out_specs = P("seq", "tp")
    return jax.shard_map(shards, mesh=mesh, in_specs=in_specs, out_specs=out_specs, check_vma=False)
```

```python
import functools
import math

import jax
import jax.numpy as jnp
from jax import lax
from jax.experimental import pallas as pl
from jax.experimental.pallas import tpu as pltpu
from jax.sharding import PartitionSpec as P

HEAD_DIM = 128
EPSILON = 1e-05
MESH = pl.DeviceIdType.MESH
F32 = jnp.float32
BF16 = jnp.bfloat16
N_SEQ = 16
N_TP = 8


def norm_rows(values):
    row_mean = jnp.mean(values, axis=-1, keepdims=True)
    centred = values - row_mean
    variance = jnp.mean(centred * centred, axis=-1, keepdims=True)
    return centred * lax.rsqrt(variance + EPSILON)


def dot(a, b):
    return jnp.dot(a, b, preferred_element_type=F32)


def dot_t(a, b):
    return lax.dot_general(a, b, (((1,), (1,)), ((), ())), preferred_element_type=F32)


class Sems:
    def __init__(self, send, recv):
        self.send, self.recv, self.used = send, recv, 0

    def take(self, count):
        first = self.used
        self.used += count
        return first


class RingGather:
    def __init__(self, sems, ring, pair, block, device, half=None):
        self.sems, self.ring, self.pair, self.half = sems, ring, pair, half
        self.block, self.device = block, device
        self.base = sems.take(8)
        self.sent = []

    def _copy(self, i, ring, pair, device):
        ref = self.block(ring, pair)
        if self.half is not None and i in (3, 7):
            ref = self.half(ref, i // 7)
        return pltpu.make_async_remote_copy(
            src_ref=ref,
            dst_ref=ref,
            send_sem=self.sems.send.at[self.base + i],
            recv_sem=self.sems.recv.at[self.base + i],
            device_id=device,
            device_id_type=MESH,
        )

    def _send(self, i, ring, pair, to_ring, to_pair):
        copy = self._copy(i, ring, pair, self.device(to_ring, to_pair))
        copy.start()
        self.sent.append(copy)

    def _wait(self, i, ring, pair):
        self._copy(i, ring, pair, self.device(self.ring, 1 - self.pair)).wait_recv()

    def start(self):
        r, p = self.ring, self.pair
        self._send(0, r, p, r, 1 - p)
        self._send(1, r, p, r + 1, p)
        self._send(2, r, p, r + 3, p)
        if self.half is None:
            self._send(3, r, p, r + 2, p)

    def partner(self):
        r, p = self.ring, self.pair
        self._wait(0, r, 1 - p)
        self._send(4, r, 1 - p, r + 1, p)
        self._send(5, r, 1 - p, r + 3, p)

    def sides(self):
        r, p = self.ring, self.pair
        self._wait(1, r + 3, p)
        if self.half is not None:
            self._send(3, r + 3, p, r + 1, p)
        self._wait(2, r + 1, p)
        if self.half is not None:
            self._send(7, r + 1, p, r + 3, p)

    def far(self):
        r, p = self.ring, self.pair
        self._wait(3, r + 2, p)
        if self.half is not None:
            self._wait(7, r + 2, p)
        self._send(6, r + 2, p, r, 1 - p)

    def partner_sides(self):
        self._wait(4, self.ring + 3, 1 - self.pair)
        self._wait(5, self.ring + 1, 1 - self.pair)

    def partner_far(self):
        self._wait(6, self.ring + 2, 1 - self.pair)

    def drain(self):
        for copy in self.sent:
            copy.wait_send()


class CoreShare:
    def __init__(self, sems, block, core, device):
        self.sems, self.block, self.core, self.device = sems, block, core, device
        self.base = sems.take(8)
        self.sent = []

    def _copy(self, i, ring, pair, core):
        ref = self.block(ring, pair, core)
        return pltpu.make_async_remote_copy(
            src_ref=ref,
            dst_ref=ref,
            send_sem=self.sems.send.at[self.base + i],
            recv_sem=self.sems.recv.at[self.base + i],
            device_id=self.device,
            device_id_type=MESH,
        )

    def send(self, i, ring, pair):
        copy = self._copy(i, ring, pair, self.core)
        copy.start()
        self.sent.append(copy)

    def wait(self, i, ring, pair):
        self._copy(i, ring, pair, 1 - self.core).wait_recv()

    def drain(self):
        for copy in self.sent:
            copy.wait_send()


def kernel(
    vis_tile,
    vis_row,
    tok_hbm,
    w_in_hbm,
    w_out_hbm,
    w_q_hbm,
    w_k_hbm,
    w_v_hbm,
    w_p_hbm,
    out_ref,
    tok,
    w_in,
    w_out,
    w_q,
    w_k,
    w_v,
    w_p,
    counts,
    pick_out,
    pick_in,
    own_rows,
    enc_in,
    hidden,
    part_out,
    far_in,
    both_out,
    side_in,
    pair_out,
    pair_in,
    key_in,
    kv,
    q_ref,
    top_ref,
    acc_ref,
    att_out,
    att_in,
    proj,
    res_out,
    res_in,
    stat_out,
    stat_in,
    own_cols,
    result,
    local_sem,
    send_sem,
    recv_sem,
):
    rows, width = tok.shape
    seq = lax.axis_index("seq")
    tp = lax.axis_index("tp")
    core, z_lo, y = seq % 2, (seq // 2) % 2, seq // 4
    x, z_hi = tp // 2, tp % 2
    sems = Sems(send_sem, recv_sem)
    block_rows = own_rows.shape[0] // 2
    group = block_rows * N_TP
    half_width = width // 2

    def at_seq(index):
        return {"seq": index, "tp": tp}

    def at_tp(index):
        return {"seq": seq, "tp": index}

    def seq_of(ring, pair, which):
        return ((ring % 4) * 2 + pair) * 2 + which

    def tp_of(ring, pair):
        return (ring % 4) * 2 + pair

    slice_rows = w_p.shape[2] // 8

    def slice_of(ring, which):
        return pl.ds(pl.multiple_of(((ring % 4) * 2 + which) * slice_rows, slice_rows), slice_rows)

    own_slice = slice_of(y, core)
    loads = [
        pltpu.make_async_copy(src, dst, local_sem.at[i])
        for i, (src, dst) in enumerate(
            (
                (tok_hbm, tok),
                (w_p_hbm.at[own_slice], w_p.at[z_hi, x, own_slice]),
                (w_q_hbm, w_q),
                (w_in_hbm, w_in),
                (w_out_hbm, w_out),
                (w_k_hbm, w_k),
                (w_v_hbm, w_v),
            )
        )
    ]
    got_tok, got_p, got_q, got_in, got_out, got_k, got_v = loads
    for copy in loads[:2]:
        copy.start()

    barrier = pltpu.get_barrier_semaphore()

    @pl.loop(1, N_SEQ)
    def _(d):
        pl.semaphore_signal(
            barrier, inc=1, device_id=at_seq((seq + d) % N_SEQ), device_id_type=MESH
        )

    @pl.loop(1, N_TP)
    def _(d):
        pl.semaphore_signal(barrier, inc=1, device_id=at_tp((tp + d) % N_TP), device_id_type=MESH)

    visible = vis_row[...].astype(F32)
    lower = (
        lax.broadcasted_iota(jnp.int32, (rows, rows), 0)
        <= lax.broadcasted_iota(jnp.int32, (rows, rows), 1)
    ).astype(F32).astype(BF16)
    upto = dot(jnp.broadcast_to(visible, (8, rows)).astype(BF16), lower)[:1]

    pl.semaphore_wait(barrier, N_SEQ + N_TP - 2)

    def remote(src, dst, index, device):
        return pltpu.make_async_remote_copy(
            src_ref=src,
            dst_ref=dst,
            send_sem=send_sem.at[index],
            recv_sem=recv_sem.at[index],
            device_id=device,
            device_id_type=MESH,
        )

    count_base = sems.take(N_SEQ)

    @pl.loop(1, N_SEQ)
    def _(d):
        far_first = (d + 6) % (N_SEQ - 1) + 1
        remote(
            vis_tile, counts.at[seq], count_base + far_first, at_seq((seq + far_first) % N_SEQ)
        ).start()

    counts[pl.ds(seq, 1)] = vis_tile[...][None]

    slice_base = sems.take(8)
    pair_device = at_tp(tp_of(x, 1 - z_hi))
    remote(
        w_p_hbm.at[own_slice], w_p.at[z_hi, x, own_slice], slice_base, pair_device
    ).start()

    def slice_copy(of, d, ring):
        here = w_p.at[of, ring, own_slice]
        src = w_p_hbm.at[own_slice] if of is z_hi else w_p.at[of, x, own_slice]
        index = slice_base + d + (0 if of is z_hi else 4)
        return remote(src, here, index, at_tp(tp_of(x + d, z_hi)))

    @pl.loop(1, 4)
    def _(d):
        slice_copy(z_hi, d, x).start()

    @pl.loop(1, N_SEQ)
    def _(d):
        remote(
            vis_tile, counts.at[(seq + N_SEQ - d) % N_SEQ], count_base + d, at_seq((seq + d) % N_SEQ)
        ).wait()

    lane_source = lax.broadcasted_iota(jnp.int32, (1, 256), 1) // 16
    before_me = jnp.zeros((1, 1), F32)
    lane_before = jnp.zeros((1, 256), F32)
    lane_count = jnp.zeros((1, 256), F32)
    for s in range(N_SEQ):
        count = jnp.sum(counts[s].astype(F32), axis=1, keepdims=True)
        count = jnp.sum(count, axis=0, keepdims=True)
        before_me = before_me + jnp.where(seq > s, 1.0, 0.0) * count
        lane_before = lane_before + jnp.where(lane_source > s, count, 0.0)
        lane_count = lane_count + jnp.where(lane_source == s, count, 0.0)

    rank = (before_me + upto - 1.0).astype(jnp.int32)
    code = ((rank >> 3) & 15) * 8 + ((rank >> 7) & 7)
    code = jnp.where((visible > 0.0) & ((rank & 7) == tp), code, -1)
    picks = (lax.broadcasted_iota(jnp.int32, (128, rows), 0) == code).astype(F32).astype(BF16)
    got_tok.wait()
    for h in range(2):
        for c in range(0, half_width, 640):
            rows_of = dot(picks, tok[:, h * half_width + c : h * half_width + c + 640])
            rows_of = rows_of.reshape(16, 8, 640)
            if h == 0:
                proj[:, c : c + 640] = rows_of.reshape(128, 640)
            else:
                first = proj[:, c : c + 640].reshape(16, 8, 640)
                both = jnp.concatenate([first, rows_of], axis=1)
                pick_out[:, c : c + 640] = both.reshape(256, 640).astype(BF16)

    pick_base = sems.take(N_SEQ)

    def pick_rows(index):
        return pl.ds(pl.multiple_of(index * 16, 16), 16)

    @pl.loop(1, N_SEQ)
    def _(d):
        far_first = (d + 6) % (N_SEQ - 1) + 1
        to = (seq + far_first) % N_SEQ
        remote(
            pick_out.at[pick_rows(to)], pick_in.at[pick_rows(seq)], pick_base + far_first, at_seq(to)
        ).start()

    pick_in[pick_rows(seq)] = pick_out[pick_rows(seq)]
    other_z = 1 - z_hi
    remote(
        w_p_hbm.at[own_slice], w_p.at[other_z, x, own_slice], slice_base, pair_device
    ).wait()

    @pl.loop(1, 4)
    def _(d):
        slice_copy(other_z, d, x).start()

    for copy in loads[2:]:
        copy.start()

    query_scale = HEAD_DIM ** (-0.5) * math.log2(math.e)
    got_q.wait()

    def make_queries(first, last):
        @pl.loop(first, last)
        def _(c):
            here = pl.ds(pl.multiple_of(c * 128, 128), 128)
            normed = norm_rows(tok[here].astype(F32)).astype(BF16)
            q_ref[here] = (dot(normed, w_q[...]) * query_scale).astype(BF16)

    make_queries(0, 4)

    @pl.loop(1, N_SEQ)
    def _(d):
        to = (seq + d) % N_SEQ
        source = (seq + N_SEQ - d) % N_SEQ
        remote(
            pick_out.at[pick_rows(to)], pick_in.at[pick_rows(source)], pick_base + d, at_seq(to)
        ).wait()

    slot = lax.broadcasted_iota(jnp.int32, (2 * block_rows, 256), 0)
    lane = lax.broadcasted_iota(jnp.int32, (2 * block_rows, 256), 1)
    wanted = (slot * 128 + seq * 8 + tp).astype(F32)
    live = (wanted >= lane_before) & (wanted < lane_before + lane_count)
    live = live & ((lane & 7) == (slot & 7))
    for h in range(2):
        chosen = (live & (((lane >> 3) & 1) == h)).astype(F32).astype(BF16)
        own_rows[:, h * half_width : (h + 1) * half_width] = dot(chosen, pick_in[...])

    def own_block(ref, a, ring, pair):
        first = tp_of(ring, pair) * block_rows
        return ref.at[a, pl.ds(pl.multiple_of(first, block_rows), block_rows)]

    def tp_device(ring, pair):
        return at_tp(tp_of(ring, pair))

    mine = pl.ds(pl.multiple_of(tp * block_rows, block_rows), block_rows)
    halves = [slice(a * block_rows, (a + 1) * block_rows) for a in range(2)]
    gather_in = []
    for a in range(2):
        enc_in[a, mine] = norm_rows(own_rows[halves[a]]).astype(BF16)
        gather_in.append(
            RingGather(sems, x, z_hi, functools.partial(own_block, enc_in, a), tp_device)
        )
        gather_in[a].start()

    def seq_device(ring, pair):
        return at_seq(seq_of(ring, pair, core))

    other_core = at_seq(seq_of(y, z_lo, 1 - core))
    up, down = seq_device(y + 1, z_lo), seq_device(y + 3, z_lo)
    w_base = sems.take(11)

    def w_copy(i, ring, which=None):
        ref = w_p.at[:, :, slice_of(ring, core if which is None else which)]
        return remote(ref, ref, w_base + i, (up, down)[i] if i < 2 else other_core)

    def w_part(i, ring):
        ref = w_p.at[i, x, slice_of(ring, core)]
        return remote(ref, ref, w_base + 2 + i, (up, down)[i])

    def w_cross(d, block):
        ref = w_p.at[:, block, slice_of(y + 2, core)]
        return remote(ref, ref, w_base + 7 + d, at_tp(tp_of(x + d, z_hi)))

    def w_start():
        got_p.wait()

        @pl.loop(1, 4)
        def _(d):
            slice_copy(z_hi, d, (x + 4 - d) % 4).wait()

        @pl.loop(1, 4)
        def _(d):
            slice_copy(other_z, d, (x + 4 - d) % 4).wait()

        w_copy(0, y).start()
        w_copy(1, y).start()
        w_copy(4, y).start()

    def w_sides():
        w_copy(0, y + 3).wait_recv()
        w_part(0, y + 3).start()
        w_copy(5, y + 3).start()
        w_copy(1, y + 1).wait_recv()
        w_part(1, y + 1).start()
        w_copy(6, y + 1).start()

    def w_spread():
        w_part(0, y + 2).wait_recv()
        w_part(1, y + 2).wait_recv()

        @pl.loop(1, 4)
        def _(d):
            w_cross(d, x).start()

    def w_far():
        @pl.loop(1, 4)
        def _(d):
            w_cross(d, (x + 4 - d) % 4).wait_recv()

        w_copy(7, y + 2).start()
        for i, ring in enumerate((y, y + 3, y + 1, y + 2)):
            w_copy(4 + i, ring, 1 - core).wait_recv()

    def w_drain():
        for i, ring in ((0, y), (1, y), (4, y), (5, y + 3), (6, y + 1), (7, y + 2)):
            w_copy(i, ring).wait_send()
        w_part(0, y + 3).wait_send()
        w_part(1, y + 1).wait_send()

        @pl.loop(1, 4)
        def _(d):
            w_cross(d, x).wait_send()

    def to_hidden(a):
        @pl.loop(0, hidden.shape[2] // 256)
        def _(c):
            here = pl.ds(pl.multiple_of(c * 256, 256), 256)
            hidden[a, :, here] = jax.nn.gelu(dot(enc_in[a], w_in[:, here])).astype(BF16)

    def to_part(a):
        @pl.loop(0, width // 256)
        def _(c):
            here = pl.ds(pl.multiple_of(c * 256, 256), 256)
            part_out[a, :, here] = dot(hidden[a], w_out[:, here]).astype(BF16)

    slab_rows = 2 * block_rows
    low, high = pl.ds(0, half_width), pl.ds(half_width, half_width)
    sum_base = [sems.take(7), sems.take(7)]
    right, left = at_tp(tp_of(x + 1, z_hi)), at_tp(tp_of(x + 3, z_hi))

    def slab(ring):
        return pl.ds(pl.multiple_of((ring % 4) * slab_rows, slab_rows), slab_rows)

    def of_pair(pair):
        return pl.ds(pl.multiple_of(pair * block_rows, block_rows), block_rows)

    def of_both(pair):
        first = (x * 2 + pair) * block_rows
        return pl.ds(pl.multiple_of(first, block_rows), block_rows)

    def sum_copy(a, i):
        part, side = part_out.at[a], side_in.at[a]
        src, dst, to = (
            lambda: (part.at[slab(x + 2), low], far_in.at[a, 0], right),
            lambda: (part.at[slab(x + 2), high], far_in.at[a, 1], left),
            lambda: (part.at[slab(x + 1), high], side.at[0, :, high], right),
            lambda: (part.at[slab(x + 3), low], side.at[1, :, low], left),
            lambda: (both_out.at[a, 0], side.at[0, :, low], right),
            lambda: (both_out.at[a, 1], side.at[1, :, high], left),
            lambda: (pair_out.at[a], pair_in.at[a], at_tp(tp_of(x, 1 - z_hi))),
        )[i]()
        return remote(src, dst, sum_base[a] + i, to)

    def sum_start(a):
        for i in range(2):
            sum_copy(a, i).start()

    def sum_sides(a):
        for i in range(2, 4):
            sum_copy(a, i).start()

    def sum_add(a):
        for i, (ring, columns) in enumerate(((x + 1, low), (x + 3, high))):
            sum_copy(a, i).wait_recv()
            own = part_out[a, slab(ring), columns].astype(F32)
            both_out[a, i] = (own + far_in[a, i].astype(F32)).astype(BF16)
            sum_copy(a, 4 + i).start()

    def sum_of_pair(a, pair):
        total = part_out[a, of_both(pair)].astype(F32)
        return total + sum(side_in[a, i, of_pair(pair)].astype(F32) for i in range(2))

    def sum_swap(a):
        for i in range(2, 6):
            sum_copy(a, i).wait_recv()
        pair_out[a] = sum_of_pair(a, 1 - z_hi).astype(BF16)
        sum_copy(a, 6).start()

    gather_key = [
        RingGather(sems, x, z_hi, functools.partial(own_block, key_in, a), tp_device)
        for a in range(2)
    ]

    def sum_end(a):
        total = own_rows[halves[a]] + sum_of_pair(a, z_hi)
        sum_copy(a, 6).wait_recv()
        encoded = (total + pair_in[a].astype(F32)).astype(BF16).astype(F32)
        key_in[a, mine] = norm_rows(encoded).astype(BF16)
        gather_key[a].start()

    kv_width = w_k.shape[1]
    own = seq_of(y, z_lo, core)

    def kv_block(a, ring, pair, which):
        return kv.at[seq_of(ring, pair, which), a]

    def half_of(ref, half):
        return ref.at[pl.ds(half * (group // 2), group // 2)]

    def kv_gather(a):
        return RingGather(
            sems,
            y,
            z_lo,
            lambda ring, pair: kv_block(a, ring, pair, core),
            seq_device,
            half=half_of if a == 0 else None,
        )

    gather_kv = [kv_gather(a) for a in range(2)]
    share_kv = [
        CoreShare(sems, functools.partial(kv_block, a), core, other_core) for a in range(2)
    ]

    def to_kv(a):
        kv[own, a, :, :kv_width] = dot(key_in[a], w_k[...]).astype(BF16)
        kv[own, a, :, kv_width:] = dot(key_in[a], w_v[...]).astype(BF16)
        gather_kv[a].start()
        share_kv[a].send(0, y, z_lo)

    def kv_partner(a):
        gather_kv[a].partner()
        share_kv[a].send(1, y, 1 - z_lo)

    def kv_sides(a):
        gather_kv[a].sides()
        share_kv[a].send(2, y + 3, z_lo)
        share_kv[a].send(3, y + 1, z_lo)

    def kv_partner_sides(a):
        gather_kv[a].partner_sides()
        share_kv[a].send(4, y + 3, 1 - z_lo)
        share_kv[a].send(5, y + 1, 1 - z_lo)

    def kv_far(a):
        gather_kv[a].far()
        share_kv[a].send(6, y + 2, z_lo)

    def kv_partner_far(a):
        gather_kv[a].partner_far()
        share_kv[a].send(7, y + 2, 1 - z_lo)

    ones = jnp.ones((group, HEAD_DIM), BF16)

    def attend(here, a, blocks):
        for h in range(2):
            cols = slice(h * HEAD_DIM, (h + 1) * HEAD_DIM)
            v_cols = slice(kv_width + h * HEAD_DIM, kv_width + (h + 1) * HEAD_DIM)
            keys = jnp.concatenate([kv[b, a, :, cols] for b in blocks], axis=0)
            values = jnp.concatenate(
                [jnp.concatenate([kv[b, a, :, v_cols], ones], axis=1) for b in blocks], axis=0
            )
            scores = dot_t(q_ref[here, cols], keys)
            old = top_ref[h, here]
            new = jnp.maximum(old, jnp.max(scores, axis=1, keepdims=True))
            shrink = jnp.exp2(old - new)
            spread = jnp.concatenate([new] * (scores.shape[1] // HEAD_DIM), axis=1)
            weights = jnp.exp2(scores - spread)
            top_ref[h, here] = new
            acc_ref[h, here] = acc_ref[h, here] * jnp.concatenate([shrink] * 2, axis=1) + dot(
                weights.astype(BF16), values
            )

    pairs = (
        ((y, z_lo), (y, 1 - z_lo)),
        ((y + 3, z_lo), (y + 1, z_lo)),
        ((y + 3, 1 - z_lo), (y + 1, 1 - z_lo)),
        ((y + 2, z_lo), (y + 2, 1 - z_lo)),
    )

    def blocks_of(step):
        places = pairs[2 * step] + pairs[2 * step + 1]
        return [seq_of(*place, c) for place in places for c in (core, 1 - core)]

    def share_wait(a, step):
        for i in range(4):
            share_kv[a].wait(4 * step + i, *pairs[2 * step + i // 2][i % 2])

    def attend_all(a, step):
        share_wait(a, step)
        blocks = blocks_of(step)

        @pl.loop(0, rows // 512)
        def _(c):
            attend(pl.ds(pl.multiple_of(c * 512, 512), 512), a, blocks)


    def transpose_own():
        part = width // N_TP
        both_cols = pl.ds(pl.multiple_of(x * 2 * part, 2 * part), 2 * part)

        @pl.loop(0, rows // 128)
        def _(c):
            here = pl.ds(pl.multiple_of(c * 128, 128), 128)
            wide = tok[here, both_cols].astype(F32)
            own_cols[:, here] = jnp.where(z_hi == 0, wide[:, :part], wide[:, part:]).T.astype(BF16)

    make_queries(4, 6)
    w_start()
    gather_in[0].partner()
    gather_in[0].sides()
    gather_in[0].far()
    gather_in[1].partner()
    gather_in[1].sides()
    gather_in[1].far()
    gather_in[0].partner_sides()
    got_in.wait()
    gather_in[0].partner_far()
    to_hidden(0)
    got_out.wait()
    to_part(0)
    sum_start(0)
    gather_in[1].partner_sides()
    gather_in[1].partner_far()
    to_hidden(1)
    sum_sides(0)
    to_part(1)
    sum_add(0)
    sum_start(1)
    sum_swap(0)
    sum_sides(1)
    sum_add(1)
    sum_end(0)
    sum_swap(1)
    make_queries(6, 8)
    transpose_own()
    gather_key[0].partner()
    gather_key[0].sides()
    gather_key[0].far()
    sum_end(1)
    w_sides()
    gather_key[0].partner_sides()
    got_k.wait()
    got_v.wait()
    gather_key[0].partner_far()
    to_kv(0)
    gather_key[1].partner()
    gather_key[1].sides()
    gather_key[1].far()
    kv_sides(0)
    kv_partner(0)
    kv_far(0)
    gather_key[1].partner_sides()
    gather_key[1].partner_far()
    to_kv(1)
    w_spread()
    top_ref[...] = jnp.full(top_ref.shape, -1e30, F32)
    acc_ref[...] = jnp.zeros(acc_ref.shape, F32)
    kv_partner_sides(0)
    kv_partner_far(0)
    attend_all(0, 0)
    kv_partner(1)
    kv_sides(1)
    kv_far(1)
    attend_all(0, 1)
    kv_partner_sides(1)
    kv_partner_far(1)
    attend_all(1, 0)
    share_wait(1, 1)

    att_base = sems.take(8)
    last_blocks = blocks_of(1)

    def att_copy(i, b, to, source, of):
        return pltpu.make_async_remote_copy(
            src_ref=att_out.at[to],
            dst_ref=att_in.at[source],
            send_sem=send_sem.at[att_base + i * 2 + b],
            recv_sem=recv_sem.at[att_base + i * 2 + of],
            device_id=at_tp(to),
            device_id_type=MESH,
        )

    @pl.loop(0, 4)
    def _(i):
        ring = (x + 1 + i) % 4
        here = pl.ds(pl.multiple_of(ring * 256, 256), 256)
        attend(here, 1, last_blocks)
        for h in range(2):
            done = acc_ref[h, here]
            done = (done[:, :HEAD_DIM] / done[:, HEAD_DIM:]).astype(BF16)
            cols = slice(h * HEAD_DIM, (h + 1) * HEAD_DIM)
            att_out[pl.ds(tp_of(ring, 0), 2), :, cols] = done.reshape(2, 128, HEAD_DIM)

        @pl.when(i < 3)
        def _():
            for b in range(2):
                att_copy(i, b, tp_of(ring, b), tp, z_hi).start()

    to_pair = tp_of(x, 1 - z_hi)
    att_copy(3, 0, to_pair, tp, 0).start()
    att_in[pl.ds(tp, 1)] = att_out[pl.ds(tp, 1)]

    w_far()

    @pl.loop(0, 3)
    def _(i):
        for b in range(2):
            to = tp_of(x + 1 + i, b)
            source = tp_of(x + 3 - i, b)
            copy = att_copy(i, b, to, source, b)
            copy.wait_send()
            copy.wait_recv()

    att_copy(3, 0, to_pair, to_pair, 0).wait()

    part = width // N_TP
    res_base = sems.take(8)
    stat_base = sems.take(N_TP)

    def res_copy(i, b, to, source, of):
        return pltpu.make_async_remote_copy(
            src_ref=res_out.at[to],
            dst_ref=res_in.at[source],
            send_sem=send_sem.at[res_base + i * 2 + b],
            recv_sem=recv_sem.at[res_base + i * 2 + of],
            device_id=at_tp(to),
            device_id_type=MESH,
        )

    @pl.loop(0, 4)
    def _(i):
        ring = (x + 1 + i) % 4
        here = pl.ds(pl.multiple_of(ring * 2 * part, 2 * part), 2 * part)
        total = dot(att_in[0], w_p[0, 0, :, here])
        for t in range(1, N_TP):
            total = total + dot(att_in[t], w_p[t % 2, t // 2, :, here])
        proj[:, here] = total
        for b in range(2):
            block = total[:, b * part : (b + 1) * part].T.astype(BF16)
            res_out[pl.ds(tp_of(ring, b), 1)] = block[None]

        @pl.when(i < 3)
        def _():
            for b in range(2):
                res_copy(i, b, tp_of(ring, b), tp, z_hi).start()

    res_copy(3, 0, to_pair, tp, 0).start()
    res_in[pl.ds(tp, 1)] = res_out[pl.ds(tp, 1)]
    row_mean = jnp.mean(proj[...], axis=1, keepdims=True)
    centred = proj[...] - row_mean
    scale = lax.rsqrt(jnp.mean(centred * centred, axis=1, keepdims=True) + EPSILON)
    lane = lax.broadcasted_iota(jnp.int32, (HEAD_DIM, HEAD_DIM), 1)
    stat_out[...] = jnp.where(lane == 0, row_mean, scale).T[:8]

    def stat_copy(d, source):
        return remote(stat_out, stat_in.at[source], stat_base + d, at_tp((tp + d) % N_TP))

    @pl.loop(1, N_TP)
    def _(d):
        stat_copy(d, tp).start()

    stat_in[pl.ds(tp, 1)] = stat_out[...][None]

    def finish(source):
        here = pl.ds(pl.multiple_of(source * HEAD_DIM, HEAD_DIM), HEAD_DIM)
        stats = stat_in[source]
        normal = (res_in[source].astype(F32) - stats[:1]) * stats[1:2]
        result[:, here] = own_cols[:, here].astype(F32) + normal
        copy = pltpu.make_async_copy(
            result.at[:, here], out_ref.at[:, here], local_sem.at[8 + source]
        )
        copy.start()

    finish(tp)

    @pl.loop(1, N_TP)
    def _(d):
        stat_copy(d, (tp + N_TP - d) % N_TP).wait()

    res_copy(3, 0, to_pair, to_pair, 0).wait()
    finish(to_pair)

    @pl.loop(0, 3)
    def _(i):
        for b in range(2):
            source = tp_of(x + 3 - i, b)
            copy = res_copy(i, b, tp_of(x + 1 + i, b), source, b)
            copy.wait_send()
            copy.wait_recv()
            finish(source)

    @pl.loop(0, N_TP)
    def _(t):
        here = pl.ds(pl.multiple_of(t * HEAD_DIM, HEAD_DIM), HEAD_DIM)
        pltpu.make_async_copy(
            result.at[:, here], out_ref.at[:, here], local_sem.at[8 + t]
        ).wait()

    for transfer in (*gather_in, *gather_key, *gather_kv, *share_kv):
        transfer.drain()
    for a in range(2):
        for i in range(7):
            sum_copy(a, i).wait_send()
    w_drain()


def shards(tokens, visible, w_in, w_out, w_query, w_key, w_value, w_proj):
    rows, width = tokens.shape
    part = width // N_TP
    block_rows = rows // 64
    group = block_rows * N_TP
    any_spec = pl.BlockSpec(memory_space=pl.ANY)
    vmem_spec = pl.BlockSpec(memory_space=pltpu.VMEM)
    heads = w_query.shape[1]
    result = pl.pallas_call(
        kernel,
        out_shape=jax.ShapeDtypeStruct((part, rows), F32),
        in_specs=[vmem_spec] * 2 + [any_spec] * 7,
        out_specs=any_spec,
        scratch_shapes=[
            pltpu.VMEM(tokens.shape, BF16),
            pltpu.VMEM(w_in.shape, BF16),
            pltpu.VMEM(w_out.shape, BF16),
            pltpu.VMEM(w_query.shape, BF16),
            pltpu.VMEM(w_key.shape, BF16),
            pltpu.VMEM(w_value.shape, BF16),
            pltpu.VMEM((2, 4, *w_proj.shape), BF16),
            pltpu.VMEM((N_SEQ, 8, rows // 8), jnp.int32),
            pltpu.VMEM((16 * N_SEQ, width // 2), BF16),
            pltpu.VMEM((16 * N_SEQ, width // 2), BF16),
            pltpu.VMEM((2 * block_rows, width), F32),
            pltpu.VMEM((2, group, width), BF16),
            pltpu.VMEM((2, group, w_in.shape[1]), BF16),
            pltpu.VMEM((2, group, width), BF16),
            pltpu.VMEM((2, 2, 2 * block_rows, width // 2), BF16),
            pltpu.VMEM((2, 2, 2 * block_rows, width // 2), BF16),
            pltpu.VMEM((2, 2, 2 * block_rows, width), BF16),
            pltpu.VMEM((2, block_rows, width), BF16),
            pltpu.VMEM((2, block_rows, width), BF16),
            pltpu.VMEM((2, group, width), BF16),
            pltpu.VMEM((N_SEQ, 2, group, 2 * heads), BF16),
            pltpu.VMEM((rows, heads), BF16),
            pltpu.VMEM((2, rows, HEAD_DIM), F32),
            pltpu.VMEM((2, rows, 2 * HEAD_DIM), F32),
            pltpu.VMEM((N_TP, rows // N_TP, heads), BF16),
            pltpu.VMEM((N_TP, rows // N_TP, heads), BF16),
            pltpu.VMEM((rows // N_TP, width), F32),
            pltpu.VMEM((N_TP, part, rows // N_TP), BF16),
            pltpu.VMEM((N_TP, part, rows // N_TP), BF16),
            pltpu.VMEM((8, rows // N_TP), F32),
            pltpu.VMEM((N_TP, 8, rows // N_TP), F32),
            pltpu.VMEM((part, rows), BF16),
            pltpu.VMEM((part, rows), F32),
            pltpu.SemaphoreType.DMA((16,)),
            pltpu.SemaphoreType.DMA((160,)),
            pltpu.SemaphoreType.DMA((160,)),
        ],
        compiler_params=pltpu.CompilerParams(
            collective_id=0, has_side_effects=True, vmem_limit_bytes=60 * 1024 * 1024
        ),
        name="generator_step",
    )(
        visible.reshape(8, rows // 8),
        visible.reshape(1, rows),
        tokens,
        w_in,
        w_out,
        w_query,
        w_key,
        w_value,
        w_proj,
    )
    return result.T


def solution(mesh):
    in_specs = (
        P("seq", None),
        P("seq"),
        P(None, "tp"),
        P("tp", None),
        P(None, "tp"),
        P(None, "tp"),
        P(None, "tp"),
        P("tp", None),
    )
    out_specs = P("seq", "tp")
    return jax.shard_map(shards, mesh=mesh, in_specs=in_specs, out_specs=out_specs, check_vma=False)
```
